32 devices in a mesh: groups: 2 (over x), ctx: 4 (over y, core), chan: 4 (over z).
Axes of the slice: x: 2, y: 2, z: 4, core: 2. Of those that a mesh axis runs over, the one named last changes fastest.
Arguments:
- stretch_rows: bfloat16 [96, 16, 3, 8192], P(('groups', 'ctx'), None, None, 'chan'), parts along dimension 0, may hold values from -6 to 6
- stretch_owner: int32 [96], P(('groups', 'ctx')), parts along dimension 0, may hold values from 0 to 3, as said below
- send_slot: int32 [8, 4, 6], P(('groups', 'ctx')), parts along dimension 0, may hold values from -1 to 15, as said below
- decode_rows: bfloat16 [128, 3, 8192], P(('groups', 'ctx'), None, 'chan'), parts along dimension 0, may hold values from -6 to 6
- row_owner: int32 [128], P(('groups', 'ctx')), parts along dimension 0, may hold values from 0 to 3, as said below
- row_slot: int32 [128], P(('groups', 'ctx')), parts along dimension 0, may hold values from 0 to 15
- cache_raw: bfloat16 [128, 6, 3, 8192], P(('groups', 'ctx'), None, None, 'chan'), parts along dimension 0, may hold values from -6 to 6
- cache_hist: bfloat16 [128, 127, 8192], P(('groups', 'ctx'), None, 'chan'), parts along dimension 0, may hold values from -6 to 6
- short_weight: bfloat16 [7, 3, 8192], P(None, None, 'chan'), may hold values from -2 to 2
- long_filter: bfloat16 [512, 128], P('chan'), may hold values from -0.5 to 0.5
Outputs:
- stretch_out: bfloat16 [96, 16, 8192], P(('groups', 'ctx'), None, 'chan'), parts along dimension 0
- decode_out: bfloat16 [128, 8192], P(('groups', 'ctx'), 'chan'), parts along dimension 0
The draws below stay inside these ranges and needn't reach their ends.
There are 2 independent parts, one for each index of `groups`. The reference program is written for one: setup_inputs(seed, part) draws one part's arguments, and reference() takes and returns one part's arrays. A program takes and returns all parts, laid end to end along the dimension named above; an argument that names none is the same for every part. Nothing has to cross between parts.
Inputs may be any that keep to these rules, and one draw needn't show every extreme that they name: `stretch_owner`: among the stretches of one ctx index at most 6 name the same owner; one owner, drawn from the seed, is named by exactly 6 stretches of every ctx index. send_slot[o, d, r] is the cache slot on owner o of the stretch of ctx index d that is the r-th (in stretch order, from 0) of that index to name owner o, and -1 where ctx index d has r or fewer such stretches. `row_owner`: among the decode rows of one ctx index at most 8 name the same owner; one owner, drawn from the seed, is named by exactly 8 rows of every ctx index.
All inputs are finite; a program needn't handle non-finite values.
Results may differ from the reference program's by a relative error of at most 0.0035.
Values may be sent and summed in bfloat16 or wider, within the bound.
No kernel may reach another device: no remote copies, remote signals or barrier semaphores. Data moves between devices by JAX's collectives and lax.ppermute only.
A program may use at most 128 MiB of HBM per device.

```python
import math
import jax
import jax.numpy as jnp
from jax import lax

D = 8192
GROUPS = 512
STAPS = 7
LTAPS = 128
NCH = 12
CLEN = 16
DEC_DEV = 16
SLOTS_DEV = 16
HCAP = 6
DCAP = 8
STRETCHES = 48
DROWS = 64
SLOTS = 64
N_CTX = 4


def route_owners(key, total_rows, per_block, peer_count, capacity):
    block_count = total_rows // per_block
    busiest = jax.random.randint(jax.random.fold_in(key, 1), (), 0, peer_count)
    candidates = (busiest + 1 + jnp.arange((peer_count - 1) * capacity) // capacity) % peer_count
    block_keys = jax.random.split(jax.random.fold_in(key, 2), block_count)

    def one_block(block_key):
        first_key, second_key = jax.random.split(block_key)
        picked = jax.random.permutation(first_key, candidates)[:per_block - capacity]
        members = jnp.concatenate([jnp.full((capacity,), busiest, jnp.int32), picked.astype(jnp.int32)])
        return jax.random.permutation(second_key, members)
    return jax.vmap(one_block)(block_keys).reshape(total_rows).astype(jnp.int32)


def stretch_plan(key):
    owners = route_owners(jax.random.fold_in(key, 11), N_CTX * NCH, NCH, N_CTX, HCAP)
    slot_ids = jax.random.randint(jax.random.fold_in(key, 12), (N_CTX * NCH,), 0, SLOTS_DEV).astype(jnp.int32)
    return (owners, slot_ids)


def draw_stretch_owner(key, part):
    owners, slot_ids = stretch_plan(key)
    return owners


def draw_send_slot(key, part):
    owners, slot_ids = stretch_plan(key)
    owner_grid = owners.reshape(N_CTX, NCH)
    slot_grid = slot_ids.reshape(N_CTX, NCH)
    same_owner = owner_grid[:, :, None] == owner_grid[:, None, :]
    earlier = jnp.arange(NCH)[None, :] < jnp.arange(NCH)[:, None]
    owner_rank = jnp.sum(same_owner & earlier[None], axis=2).astype(jnp.int32)
    device_rows = jnp.broadcast_to(jnp.arange(N_CTX, dtype=jnp.int32)[:, None], (N_CTX, NCH))
    slot_table = jnp.full((N_CTX, N_CTX, HCAP), -1, jnp.int32)
    return slot_table.at[owner_grid, device_rows, owner_rank].set(slot_grid)


def draw_row_owner(key, part):
    key = jax.random.fold_in(key, 5)
    return route_owners(key, N_CTX * DEC_DEV, DEC_DEV, N_CTX, DCAP)


def draw_long_filter(key, part):
    key = jax.random.fold_in(key, 7)
    first_key, second_key = jax.random.split(key)
    decay_rate = jnp.exp(jax.random.uniform(first_key, (GROUPS, 1), jnp.float32, math.log(1.0 / 1000.0), math.log(1.0 / 30.0)))
    base_values = jnp.clip(jax.random.normal(second_key, (GROUPS, LTAPS), jnp.float32), -4.0, 4.0)
    positions = jnp.arange(LTAPS, dtype=jnp.float32)[None, :]
    return (0.12 * base_values * jnp.exp(-decay_rate * positions)).astype(jnp.bfloat16)


def place_ends(values, key, smallest, largest):
    shape = values.shape
    index_at = [jax.random.randint(jax.random.fold_in(key, axis), (), 0, shape[axis]) for axis in range(len(shape))]
    values = values.at[tuple(index_at)].set(smallest)
    longest = shape.index(max(shape))
    index_at[longest] = (index_at[longest] + 1) % shape[longest]
    return values.at[tuple(index_at)].set(largest)


def level_of(own_key, extent, cuts, least, largest):
    def one(axis_at, blocks):
        steps = jax.random.uniform(jax.random.fold_in(jax.random.fold_in(own_key, 6), axis_at), (blocks,), jnp.float32, least / len(cuts), largest / len(cuts))
        return jnp.repeat(jnp.exp(steps), extent[axis_at] // blocks).reshape((-1,) + (1,) * (len(extent) - axis_at - 1))

    loudness = one(*cuts[0])
    for cut in cuts[1:]:
        loudness = loudness * one(*cut)
    return loudness


def centred(key, shape, scale, reach, cuts=(), held_as=jnp.bfloat16):
    level = level_of(key, shape, cuts, -0.22, 0.18) if cuts else 1.0
    result = jax.random.normal(key, shape, jnp.float32) * scale * level
    return jnp.minimum(jnp.maximum(result, -reach), reach).astype(held_as)


def setup_inputs(seed: int = 0, part: int = 0) -> dict:
    key_list = jax.random.split(jax.random.key(seed), 11)
    own_keys = jax.random.split(jax.random.fold_in(key_list[10], part), 11)
    stretch_rows = centred(own_keys[0], (STRETCHES, CLEN, 3, D), 1.0, 6.0, ((0, 4), (3, 4)))
    stretch_owner = draw_stretch_owner(jax.random.fold_in(jax.random.fold_in(key_list[10], part), 71), part)
    send_slot = draw_send_slot(jax.random.fold_in(jax.random.fold_in(key_list[10], part), 71), part)
    decode_rows = centred(own_keys[3], (DROWS, 3, D), 1.0, 6.0, ((0, 4), (2, 4)))
    row_owner = draw_row_owner(jax.random.fold_in(jax.random.fold_in(key_list[10], part), 71), part)
    row_slot = place_ends(jax.random.randint(own_keys[5], (DROWS,), 0, SLOTS_DEV), jax.random.fold_in(own_keys[5], 1), 0, SLOTS_DEV - 1).astype(jnp.int32)
    cache_raw = centred(own_keys[6], (SLOTS, 6, 3, D), 1.0, 6.0, ((0, 4), (3, 4)))
    cache_hist = centred(own_keys[7], (SLOTS, 127, D), 1.0, 6.0, ((0, 4), (2, 4)))
    short_weight = centred(key_list[8], (STAPS, 3, D), STAPS ** -0.5, 2.0, ((2, 4),))
    long_filter = draw_long_filter(jax.random.fold_in(key_list[10], 71), part)
    return dict(stretch_rows=stretch_rows, stretch_owner=stretch_owner, send_slot=send_slot, decode_rows=decode_rows, row_owner=row_owner, row_slot=row_slot, cache_raw=cache_raw, cache_hist=cache_hist, short_weight=short_weight, long_filter=long_filter)


def featurize(stretch_block, raw_state, hist_state, short_weight, long_filter):
    length = stretch_block.shape[1]
    extended = jnp.concatenate([raw_state, stretch_block], axis=1).astype(jnp.float32)
    weights = short_weight.astype(jnp.float32)
    featured = jnp.zeros(stretch_block.shape, jnp.float32)
    for tap_index in range(STAPS):
        offset_tap = STAPS - 1 - tap_index
        featured = featured + weights[tap_index] * extended[:, offset_tap:offset_tap + length]
    product = (featured[:, :, 1] * featured[:, :, 2]).astype(jnp.bfloat16)
    history = jnp.concatenate([hist_state, product], axis=1).astype(jnp.float32)
    span_width = history.shape[1]
    lag_table = jnp.arange(length)[:, None] + (LTAPS - 1) - jnp.arange(span_width)[None, :]
    in_band = (lag_table >= 0) & (lag_table < LTAPS)
    tap_values = jnp.take(long_filter.astype(jnp.float32), jnp.clip(lag_table, 0, LTAPS - 1), axis=1)
    toeplitz = jnp.where(in_band[None], tap_values, jnp.zeros_like(tap_values))
    row_count = stretch_block.shape[0]
    grouped = history.reshape(row_count, span_width, GROUPS, D // GROUPS)
    convolved = jnp.einsum("gim,nmgk->nigk", toeplitz, grouped).reshape(row_count, length, D)
    return (featured[:, :, 0] * convolved).astype(jnp.bfloat16)


def reference(stretch_rows, stretch_owner, send_slot, decode_rows, row_owner, row_slot, cache_raw, cache_hist, short_weight, long_filter):
    owner_grid = stretch_owner.reshape(N_CTX, NCH).astype(jnp.int32)
    same_owner = owner_grid[:, :, None] == owner_grid[:, None, :]
    earlier = jnp.arange(NCH)[None, :] < jnp.arange(NCH)[:, None]
    owner_rank = jnp.sum(same_owner & earlier[None], axis=2).astype(jnp.int32)
    device_rows = jnp.broadcast_to(jnp.arange(N_CTX, dtype=jnp.int32)[:, None], (N_CTX, NCH))
    slot_ids = send_slot[owner_grid, device_rows, owner_rank].astype(jnp.int32)
    state_index = (owner_grid * SLOTS_DEV + slot_ids).astype(jnp.int32)

    def per_device(pieces):
        stretch_block, indices = pieces
        raw_state = jnp.take(cache_raw, indices, axis=0)
        hist_state = jnp.take(cache_hist, indices, axis=0)
        return featurize(stretch_block, raw_state, hist_state, short_weight, long_filter)

    stretch_out = lax.map(per_device, (stretch_rows.reshape(N_CTX, NCH, CLEN, 3, D), state_index))
    stretch_out = stretch_out.reshape(STRETCHES, CLEN, D)
    decode_index = (row_owner * SLOTS_DEV + row_slot).astype(jnp.int32).reshape(N_CTX, DEC_DEV)
    decode_out = lax.map(per_device, (decode_rows.reshape(N_CTX, DEC_DEV, 1, 3, D), decode_index))
    decode_out = decode_out.reshape(DROWS, D)
    return (stretch_out, decode_out)
```

```python
import functools

import jax
import jax.numpy as jnp
from jax import lax
from jax.experimental import pallas as pl
from jax.experimental.pallas import tpu as pltpu
from jax.sharding import PartitionSpec as P

LANES = 128
F32 = jnp.float32
BF16 = jnp.bfloat16


def round_up(value, unit):
    return (value + unit - 1) // unit * unit


def one_hot(left, right):
    return jnp.where(left == right, 1.0, 0.0).astype(BF16)


def dot(left, right):
    return jnp.dot(left, right, preferred_element_type=F32)


def iota(shape, axis):
    return lax.broadcasted_iota(jnp.int32, shape, axis)


def rank_of(owner_ref, index):
    rank = jnp.int32(0)
    for earlier in range(index):
        rank += (owner_ref[earlier] == owner_ref[index]).astype(jnp.int32)
    return rank


def pick_own_group(stacked, length, per_group):
    lane_group = lax.rem(iota((length, stacked.shape[1]), 1), LANES) // per_group
    picked = stacked[:length]
    for group in range(1, LANES // per_group):
        picked = jnp.where(lane_group == group, stacked[group * length : (group + 1) * length], picked)
    return picked


def pack_kernel(peers, cap, planes, slots, dpad, me_ref, slot_ref, owner_ref, code_ref, raw_ref, rows_ref, *rest):
    outs, (raw_sel, rows_sel) = rest[:peers], rest[peers:]
    padded = raw_sel.shape[0] // peers
    decode_count = owner_ref.shape[0]
    width = raw_ref.shape[1]

    @pl.when(pl.program_id(0) == 0)
    def _():
        row = iota((padded, 1), 0)
        column = iota((padded, planes * slots), 1)
        for k in range(peers):
            target = jnp.full((padded, 1), -1, jnp.int32)
            for r in range(cap):
                slot = jnp.maximum(slot_ref[0, me_ref[0] ^ k, r], 0)
                here = (row >= r * planes) & (row < (r + 1) * planes)
                target = jnp.where(here, (row - r * planes) * slots + slot, target)
            raw_sel[k * padded : (k + 1) * padded, :] = one_hot(column, target)
        lane = iota((1, 3 * decode_count), 1)
        target = jnp.zeros((1, 3 * decode_count), jnp.int32)
        for n in range(decode_count):
            base = (owner_ref[n] ^ me_ref[0]) * (3 * dpad) + rank_of(owner_ref, n)
            for s in range(3):
                target = jnp.where(lane == s * decode_count + n, base + s * dpad, target)
        rows_sel[...] = one_hot(iota(rows_sel.shape, 0), target)

    rows = dot(rows_sel[...], rows_ref[...])
    lane = iota((padded, width), 1)
    marked = iota((padded, width), 0) == cap * planes
    for k in range(peers):
        codes = jnp.full((padded, width), -1, jnp.int32)
        for n in range(decode_count):
            place = jnp.where(owner_ref[n] ^ me_ref[0] == k, rank_of(owner_ref, n), -1)
            codes = jnp.where(lane == place, code_ref[n], codes)
        raw = dot(raw_sel[k * padded : (k + 1) * padded, :], raw_ref[...])
        raw = jnp.where(marked, codes.astype(F32), raw)
        outs[k][...] = jnp.concatenate([raw, rows[k * 3 * dpad : (k + 1) * 3 * dpad]], axis=0).astype(BF16)


def history_kernel(peers, cap, length, per_group, me_ref, slot_ref, filter_ref, hist_ref, *rest):
    sends, (first_ref, taps_ref) = rest[:peers], rest[peers : peers + 2]
    stage, toeplitz, local, states = rest[peers + 2 :]
    hist_rows, slots, _ = hist_ref.shape
    groups, taps = filter_ref.shape
    tile_rows = LANES // per_group * length

    @pl.when(pl.program_id(0) == 0)
    def _():
        source, column = iota((taps, LANES), 0), iota((taps, LANES), 1)
        for i in range(length):
            shift = jnp.where(column < hist_rows, one_hot(source, taps - 1 + i - column).astype(F32), 0.0)
            stage[pl.ds(i, groups, stride=length), :] = dot(filter_ref[...], shift.astype(BF16))
        toeplitz[...] = stage[: groups * length, :].astype(BF16)
        for i in range(length):
            stage[pl.ds(i, groups, stride=length), :] = dot(filter_ref[...], one_hot(source, i - column))
        local[...] = stage[: groups * length, :].astype(BF16)

    start = pl.multiple_of(pl.program_id(0) * tile_rows, tile_rows)
    matrix = toeplitz[pl.ds(start, tile_rows), :]
    column0 = jnp.where(iota((LANES, LANES), 0) == 0, 1.0, 0.0).astype(BF16)
    taps_ref[...] = pick_own_group(dot(local[pl.ds(start, tile_rows), :], column0), length, per_group)
    stage[: hist_rows * slots, :] = hist_ref[...].astype(F32).reshape(hist_rows * slots, LANES)
    stage[hist_rows * slots : LANES * slots, :] = jnp.zeros(((LANES - hist_rows) * slots, LANES), F32)
    for slot in range(0, slots, 2):
        pair = jnp.concatenate([stage[pl.ds(slot + e, LANES, stride=slots), :] for e in range(2)], axis=1)
        picked = pick_own_group(dot(matrix, pair.astype(BF16)), length, per_group)
        for e in range(2):
            own = picked[:, e * LANES : (e + 1) * LANES]
            states[slot + e] = own.astype(BF16)
            first_ref[slot + e : slot + e + 1, :] = own[:1]
    for k in range(peers):
        for r in range(cap):
            sends[k][r] = states[jnp.maximum(slot_ref[0, me_ref[0] ^ k, r], 0)]


def decode_kernel(peers, staps, slots, dpad, mark, padded, weight_ref, raw_ref, first_ref, taps_ref, *rest):
    rows, codes, outs = rest[:peers], rest[peers : 2 * peers], rest[2 * peers :]
    lane = iota((slots, LANES), 0)
    selects = []
    for ref in codes:
        code = ref[...].astype(F32)[mark : mark + 1].astype(jnp.int32)
        selects.append(jnp.where(lane == code, 1.0, 0.0).T[:dpad])
    select = jnp.concatenate(selects, axis=0)
    arrived = [ref[...].astype(F32)[padded:] for ref in rows]
    weight = weight_ref[...].astype(F32)
    featured = []
    for s in range(3):
        own = jnp.concatenate([block[s * dpad : (s + 1) * dpad] for block in arrived], axis=0)
        value = weight[s, 0:1] * own
        for j in range(1, staps):
            plane = (staps - 1 - j) * 3 + s
            state = dot(select.astype(BF16), raw_ref[plane * slots : (plane + 1) * slots, :])
            value += weight[s, j : j + 1] * state
        featured.append(value)
    gated = (featured[1] * featured[2]).astype(BF16).astype(F32)
    history = jnp.dot(select, first_ref[...], preferred_element_type=F32, precision=lax.Precision.HIGHEST)
    result = featured[0] * (taps_ref[0:1, :] * gated + history)
    for k in range(peers):
        outs[k][...] = result[k * dpad : (k + 1) * dpad].astype(BF16)


def local_kernel(peers, planes, staps, per_group, me_ref, owner_ref, filter_ref, weight_ref, rows_ref, *rest):
    raws, (query_ref, conv_ref) = rest[:peers], rest[peers : peers + 2]
    select, stage, local, window = rest[peers + 2 :]
    count, _, length, _ = rows_ref.shape
    groups, taps = filter_ref.shape
    padded = select.shape[1] // peers
    tile_rows = LANES // per_group * length
    lead = 8
    span = lead + length

    @pl.when(pl.program_id(0) == 0)
    def _():
        source, column = iota((taps, LANES), 0), iota((taps, LANES), 1)
        for i in range(length):
            stage[pl.ds(i, groups, stride=length), :] = dot(filter_ref[...], one_hot(source, i - column))
        local[...] = stage[...].astype(BF16)
        row = iota((lead, 1), 0) - (lead - staps + 1)
        targets = []
        for c in range(count):
            base = (owner_ref[c] ^ me_ref[0]) * padded + rank_of(owner_ref, c) * planes
            targets += [jnp.where(row >= 0, base + row * 3 + s, -1) for s in range(3)]
        select[...] = one_hot(iota(select.shape, 1), jnp.concatenate(targets, axis=0))

    start = pl.multiple_of(pl.program_id(0) * tile_rows, tile_rows)
    matrix = local[pl.ds(start, tile_rows), :][:, :length]
    lead_rows = dot(select[...], jnp.concatenate([ref[...][:padded] for ref in raws], axis=0))
    weight = weight_ref[...].astype(F32)
    for first in range(0, count, 2):
        members = range(first, min(first + 2, count))
        products = []
        for c in members:
            featured = []
            for s in range(3):
                base = ((c % 2) * 3 + s) * span
                at = (c * 3 + s) * lead
                window[base : base + lead, :] = lead_rows[at : at + lead]
                window[base + lead : base + span, :] = rows_ref[c, s].astype(F32)
                value = weight[s, 0:1] * window[base + lead : base + span, :]
                for j in range(1, staps):
                    value += weight[s, j : j + 1] * window[base + lead - j : base + span - j, :]
                featured.append(value)
            query_ref[c] = featured[0]
            products.append((featured[1] * featured[2]).astype(BF16))
        picked = pick_own_group(dot(matrix, jnp.concatenate(products, axis=1)), length, per_group)
        for e, c in enumerate(members):
            conv_ref[c] = picked[:, e * LANES : (e + 1) * LANES]


def finish_kernel(peers, cap, dpad, me_ref, owner_ref, decode_owner_ref, query_ref, conv_ref, *rest):
    states, returned = rest[:peers], rest[peers : 2 * peers]
    out_ref, decode_ref, held = rest[2 * peers :]
    count = query_ref.shape[0]
    decode_count = decode_owner_ref.shape[0]
    for k in range(peers):
        for r in range(cap):
            held[k * cap + r] = states[k][r]
    for c in range(count):
        at = (owner_ref[c] ^ me_ref[0]) * cap + rank_of(owner_ref, c)
        out_ref[c] = (query_ref[c] * (conv_ref[c] + held[at].astype(F32))).astype(BF16)
    row = iota((decode_count, 1), 0)
    target = jnp.zeros((decode_count, 1), jnp.int32)
    for n in range(decode_count):
        at = (decode_owner_ref[n] ^ me_ref[0]) * dpad + rank_of(decode_owner_ref, n)
        target = jnp.where(row == n, at, target)
    select = one_hot(iota((decode_count, peers * dpad), 1), target)
    arrived = jnp.concatenate([ref[...].astype(F32) for ref in returned], axis=0).astype(BF16)
    decode_ref[...] = dot(select, arrived).astype(BF16)


def per_device(
    stretch_rows,
    stretch_owner,
    send_slot,
    decode_rows,
    row_owner,
    row_slot,
    cache_raw,
    cache_hist,
    short_weight,
    long_filter,
):
    peers = lax.axis_size("ctx")
    cap = send_slot.shape[2]
    count, length, _, channels = stretch_rows.shape
    slots, raw_rows, _, _ = cache_raw.shape
    hist_rows = cache_hist.shape[1]
    staps = short_weight.shape[0]
    groups, taps = long_filter.shape
    per_group = channels // groups
    decode_count = decode_rows.shape[0]
    dcap = max(2, (2 * decode_count + peers - 1) // peers)
    dpad = round_up(dcap, 8)
    planes = 3 * raw_rows
    padded = round_up(planes * cap + 1, 16)
    me = lax.axis_index("ctx").astype(jnp.int32).reshape(1)

    raw2d = cache_raw.transpose(1, 2, 0, 3).reshape(planes * slots, channels)
    hist3d = cache_hist.transpose(1, 0, 2)
    rows2d = decode_rows.transpose(1, 0, 2).reshape(3 * decode_count, channels)
    stretch = stretch_rows.transpose(0, 2, 1, 3)
    weight = short_weight.transpose(1, 0, 2)

    smem = pl.BlockSpec(memory_space=pltpu.SMEM)
    params = pltpu.CompilerParams(vmem_limit_bytes=48 * 1024 * 1024)

    def tiled(width, *lead):
        return pl.BlockSpec((*lead, width), lambda t: (0,) * len(lead) + (t,))

    def whole(*shape):
        return pl.BlockSpec(shape, lambda t: (0,) * len(shape))

    def cost(flops, data):
        return pl.CostEstimate(flops=flops, bytes_accessed=data, transcendentals=0)

    def send(array, k):
        return lax.ppermute(array, "ctx", [(i, i ^ k) for i in range(peers)])

    order = sorted(range(1, peers), reverse=True)
    width = min(512, channels)
    payload = padded + 3 * dpad
    sent = list(
        pl.pallas_call(
            functools.partial(pack_kernel, peers, cap, planes, slots, dpad),
            grid=(channels // width,),
            in_specs=[smem, smem, smem, smem, tiled(width, planes * slots), tiled(width, 3 * decode_count)],
            out_specs=[tiled(width, payload)] * peers,
            out_shape=[jax.ShapeDtypeStruct((payload, channels), BF16)] * peers,
            scratch_shapes=[
                pltpu.VMEM((peers * padded, planes * slots), BF16),
                pltpu.VMEM((peers * 3 * dpad, 3 * decode_count), BF16),
            ],
            compiler_params=params,
            cost_estimate=cost(2 * peers * padded * planes * slots * channels, 5 * planes * slots * channels),
        )(me, send_slot, row_owner, row_slot, raw2d, rows2d)
    )
    for k in order:
        sent[k] = send(sent[k], k)

    tile_rows = LANES // per_group * length
    history = pl.pallas_call(
        functools.partial(history_kernel, peers, cap, length, per_group),
        grid=(channels // LANES,),
        in_specs=[smem, smem, whole(groups, taps), tiled(LANES, hist_rows, slots)],
        out_specs=[tiled(LANES, cap, length)] * peers + [tiled(LANES, slots), tiled(LANES, length)],
        out_shape=[jax.ShapeDtypeStruct((cap, length, channels), BF16)] * peers
        + [jax.ShapeDtypeStruct((slots, channels), F32), jax.ShapeDtypeStruct((length, channels), F32)],
        scratch_shapes=[
            pltpu.VMEM((max(groups * length, LANES * slots), LANES), F32),
            pltpu.VMEM((groups * length, LANES), BF16),
            pltpu.VMEM((groups * length, LANES), BF16),
            pltpu.VMEM((slots, length, LANES), BF16),
        ],
        compiler_params=params,
        cost_estimate=cost(2 * slots * tile_rows * LANES * channels, 2 * hist_rows * slots * channels),
    )(me, send_slot, long_filter, hist3d)
    states, (first, expanded) = list(history[:peers]), history[peers:]
    for k in order:
        states[k] = send(states[k], k)

    returned = list(
        pl.pallas_call(
            functools.partial(decode_kernel, peers, staps, slots, dpad, planes * cap, padded),
            grid=(channels // width,),
            in_specs=[tiled(width, 3, staps), tiled(width, planes * slots), tiled(width, slots)]
            + [tiled(width, length)]
            + [tiled(width, payload)] * peers
            + [whole(payload, LANES)] * peers,
            out_specs=[tiled(width, dpad)] * peers,
            out_shape=[jax.ShapeDtypeStruct((dpad, channels), BF16)] * peers,
            compiler_params=params,
            cost_estimate=cost(2 * peers * dpad * planes * slots * channels, 4 * planes * slots * channels),
        )(weight, raw2d, first, expanded, *sent, *sent)
    )
    for k in order:
        returned[k] = send(returned[k], k)

    query, conv = pl.pallas_call(
        functools.partial(local_kernel, peers, planes, staps, per_group),
        grid=(channels // LANES,),
        in_specs=[smem, smem, whole(groups, taps), tiled(LANES, 3, staps), tiled(LANES, count, 3, length)]
        + [tiled(LANES, payload)] * peers,
        out_specs=[tiled(LANES, count, length)] * 2,
        out_shape=[jax.ShapeDtypeStruct((count, length, channels), F32)] * 2,
        scratch_shapes=[
            pltpu.VMEM((count * 3 * 8, peers * padded), BF16),
            pltpu.VMEM((groups * length, LANES), F32),
            pltpu.VMEM((groups * length, LANES), BF16),
            pltpu.VMEM((6 * (8 + length), LANES), F32),
        ],
        compiler_params=params,
        cost_estimate=cost(2 * count * 24 * peers * padded * channels, 14 * count * length * channels),
    )(me, stretch_owner, long_filter, weight, stretch, *sent)

    return pl.pallas_call(
        functools.partial(finish_kernel, peers, cap, dpad),
        grid=(channels // width,),
        in_specs=[smem, smem, smem]
        + [tiled(width, count, length)] * 2
        + [tiled(width, cap, length)] * peers
        + [tiled(width, dpad)] * peers,
        out_specs=[tiled(width, count, length), tiled(width, decode_count)],
        out_shape=[
            jax.ShapeDtypeStruct((count, length, channels), BF16),
            jax.ShapeDtypeStruct((decode_count, channels), BF16),
        ],
        scratch_shapes=[pltpu.VMEM((peers * cap, length, width), BF16)],
        compiler_params=params,
        cost_estimate=cost(3 * count * length * channels, 14 * count * length * channels),
    )(me, stretch_owner, row_owner, query, conv, *states, *returned)


def solution(mesh):
    placed = (
        P(("groups", "ctx"), None, None, "chan"),
        P(("groups", "ctx")),
        P(("groups", "ctx"), None, None),
        P(("groups", "ctx"), None, "chan"),
        P(("groups", "ctx")),
        P(("groups", "ctx")),
        P(("groups", "ctx"), None, None, "chan"),
        P(("groups", "ctx"), None, "chan"),
        P(None, None, "chan"),
        P("chan", None),
    )
    return jax.shard_map(
        per_device,
        mesh=mesh,
        in_specs=placed,
        out_specs=(P(("groups", "ctx"), None, "chan"), P(("groups", "ctx"), "chan")),
        check_vma=False,
    )
```

```python
import functools

import jax
import jax.numpy as jnp
from jax import lax
from jax.experimental import pallas as pl
from jax.experimental.pallas import tpu as pltpu
from jax.sharding import PartitionSpec as P

LANES = 128
F32 = jnp.float32
BF16 = jnp.bfloat16


def round_up(value, unit):
    return (value + unit - 1) // unit * unit


def one_hot(left, right):
    return jnp.where(left == right, 1.0, 0.0).astype(BF16)


def dot(left, right):
    return jnp.dot(left, right, preferred_element_type=F32)


def iota(shape, axis):
    return lax.broadcasted_iota(jnp.int32, shape, axis)


def rank_of(owner_ref, index):
    rank = jnp.int32(0)
    for earlier in range(index):
        rank += (owner_ref[earlier] == owner_ref[index]).astype(jnp.int32)
    return rank


def pick_own_group(stacked, length, per_group):
    lane_group = lax.rem(iota((length, stacked.shape[1]), 1), LANES) // per_group
    picked = stacked[:length]
    for group in range(1, LANES // per_group):
        picked = jnp.where(lane_group == group, stacked[group * length : (group + 1) * length], picked)
    return picked


def pack_kernel(ks, cap, planes, slots, dpad, me_ref, slot_ref, owner_ref, code_ref, raw_hbm, rows_hbm, *rest):
    outs, (raw_ref, rows_ref, raw_sel, rows_sel, sems) = rest[: len(ks)], rest[len(ks) :]
    padded = raw_sel.shape[0] // len(ks)
    decode_count = owner_ref.shape[0]
    pairs = ((raw_hbm, raw_ref), (rows_hbm, rows_ref))
    copies = [pltpu.make_async_copy(source, target, sems.at[at]) for at, (source, target) in enumerate(pairs)]
    for copy in copies:
        copy.start()

    row = iota((padded, 1), 0)
    column = iota((padded, planes * slots), 1)
    lane = iota((1, 3 * decode_count), 1)
    wide = iota((1, LANES), 1)
    codes = []
    for at, k in enumerate(ks):
        peer = me_ref[0] ^ k
        target = jnp.full((padded, 1), -1, jnp.int32)
        for r in range(cap):
            slot = jnp.maximum(slot_ref[0, peer, r], 0)
            here = (row >= r * planes) & (row < (r + 1) * planes)
            target = jnp.where(here, (row - r * planes) * slots + slot, target)
        raw_sel[at * padded : (at + 1) * padded, :] = one_hot(column, target)
        target = jnp.full((1, 3 * decode_count), -1, jnp.int32)
        code = jnp.full((1, LANES), -1, jnp.int32)
        rank = jnp.int32(0)
        for n in range(decode_count):
            mine = owner_ref[n] == peer
            for s in range(3):
                hit = jnp.where(mine, s * decode_count + n, -1)
                target = jnp.where(lane == hit, rank + s * dpad, target)
            code = jnp.where(wide == jnp.where(mine, rank, -1), code_ref[n], code)
            rank += mine.astype(jnp.int32)
        rows_sel[at] = one_hot(iota(rows_sel.shape[1:], 0), target)
        codes.append(code.astype(F32))

    for copy in copies:
        copy.wait()
    marked = iota((padded, LANES), 0) == cap * planes
    for at in range(len(ks)):
        raw = dot(raw_sel[at * padded : (at + 1) * padded, :], raw_ref[...])
        head = jnp.where(marked, codes[at], raw[:, :LANES])
        raw = jnp.concatenate([head, raw[:, LANES:]], axis=1)
        outs[at][...] = jnp.concatenate([raw, dot(rows_sel[at], rows_ref[...])], axis=0).astype(BF16)


def history_kernel(peers, cap, length, per_group, me_ref, slot_ref, filter_ref, hist_ref, *rest):
    sends, (first_ref, taps_ref) = rest[:peers], rest[peers : peers + 2]
    stage, toeplitz, local, states = rest[peers + 2 :]
    hist_rows, slots, _ = hist_ref.shape
    groups, taps = filter_ref.shape
    tile_rows = LANES // per_group * length

    @pl.when(pl.program_id(0) == 0)
    def _():
        source, column = iota((taps, LANES), 0), iota((taps, LANES), 1)
        for i in range(length):
            shift = jnp.where(column < hist_rows, one_hot(source, taps - 1 + i - column).astype(F32), 0.0)
            stage[pl.ds(i, groups, stride=length), :] = dot(filter_ref[...], shift.astype(BF16))
        toeplitz[...] = stage[: groups * length, :].astype(BF16)
        for i in range(length):
            stage[pl.ds(i, groups, stride=length), :] = dot(filter_ref[...], one_hot(source, i - column))
        local[...] = stage[: groups * length, :].astype(BF16)

    column0 = jnp.where(iota((LANES, LANES), 0) == 0, 1.0, 0.0).astype(BF16)
    tiles = hist_ref.shape[2] // LANES
    for tile in range(tiles):
        start = pl.multiple_of((pl.program_id(0) * tiles + tile) * tile_rows, tile_rows)
        lanes = slice(tile * LANES, (tile + 1) * LANES)
        expanded = dot(local[pl.ds(start, tile_rows), :], column0)
        taps_ref[:, lanes] = pick_own_group(expanded, length, per_group)
        matrix = toeplitz[pl.ds(start, tile_rows), :]
        block = hist_ref[:, :, lanes]
        rest_rows = jnp.zeros((LANES - hist_rows, slots, LANES), BF16)
        by_slot = jnp.swapaxes(jnp.concatenate([block, rest_rows], axis=0), 0, 1)
        for slot in range(0, slots, 2):
            pair = jnp.concatenate([by_slot[slot], by_slot[slot + 1]], axis=1)
            picked = pick_own_group(dot(matrix, pair), length, per_group)
            for e in range(2):
                own = picked[:, e * LANES : (e + 1) * LANES]
                states[slot + e, :, lanes] = own.astype(BF16)
                first_ref[slot + e : slot + e + 1, lanes] = own[:1]
    for k in range(peers):
        for r in range(cap):
            sends[k][r] = states[jnp.maximum(slot_ref[0, me_ref[0] ^ k, r], 0)]


def decode_kernel(peers, staps, slots, dpad, mark, padded, weight_ref, raw_ref, first_ref, taps_ref, *rest):
    rows, codes, outs = rest[:peers], rest[peers : 2 * peers], rest[2 * peers :]
    lane = iota((slots, LANES), 0)
    selects = []
    for ref in codes:
        code = ref[...].astype(F32)[mark : mark + 1].astype(jnp.int32)
        selects.append(jnp.where(lane == code, 1.0, 0.0).T[:dpad])
    select = jnp.concatenate(selects, axis=0)
    arrived = [ref[...].astype(F32)[padded:] for ref in rows]
    weight = weight_ref[...].astype(F32)
    featured = []
    for s in range(3):
        own = jnp.concatenate([block[s * dpad : (s + 1) * dpad] for block in arrived], axis=0)
        value = weight[s, 0:1] * own
        for j in range(1, staps):
            plane = (staps - 1 - j) * 3 + s
            state = dot(select.astype(BF16), raw_ref[plane * slots : (plane + 1) * slots, :])
            value += weight[s, j : j + 1] * state
        featured.append(value)
    gated = (featured[1] * featured[2]).astype(BF16).astype(F32)
    history = jnp.dot(select, first_ref[...], preferred_element_type=F32, precision=lax.Precision.HIGHEST)
    result = featured[0] * (taps_ref[0:1, :] * gated + history)
    for k in range(peers):
        outs[k][...] = result[k * dpad : (k + 1) * dpad].astype(BF16)


def local_kernel(peers, planes, staps, per_group, me_ref, owner_ref, filter_ref, weight_ref, rows_ref, *rest):
    raws, (query_ref, conv_ref) = rest[:peers], rest[peers : peers + 2]
    select, stage, local, window = rest[peers + 2 :]
    count, _, length, _ = rows_ref.shape
    groups, taps = filter_ref.shape
    padded = select.shape[1] // peers
    tile_rows = LANES // per_group * length
    lead = 8
    span = lead + length

    @pl.when(pl.program_id(0) == 0)
    def _():
        source, column = iota((taps, LANES), 0), iota((taps, LANES), 1)
        for i in range(length):
            stage[pl.ds(i, groups, stride=length), :] = dot(filter_ref[...], one_hot(source, i - column))
        local[...] = stage[...].astype(BF16)
        row = iota((lead, 1), 0) - (lead - staps + 1)
        targets = []
        for c in range(count):
            base = (owner_ref[c] ^ me_ref[0]) * padded + rank_of(owner_ref, c) * planes
            targets += [jnp.where(row >= 0, base + row * 3 + s, -1) for s in range(3)]
        select[...] = one_hot(iota(select.shape, 1), jnp.concatenate(targets, axis=0))

    lead_rows = dot(select[...], jnp.concatenate([ref[...][:padded] for ref in raws], axis=0))
    weights = weight_ref[...].astype(F32)
    tiles = rows_ref.shape[3] // LANES
    for tile in range(tiles):
        start = pl.multiple_of((pl.program_id(0) * tiles + tile) * tile_rows, tile_rows)
        lanes = slice(tile * LANES, (tile + 1) * LANES)
        matrix = local[pl.ds(start, tile_rows), :][:, :length]
        weight = weights[:, :, lanes]
        for first in range(0, count, 2):
            members = range(first, min(first + 2, count))
            products = []
            for c in members:
                featured = []
                for s in range(3):
                    base = (((tile % 2) * count + c) * 3 + s) * span
                    at = (c * 3 + s) * lead
                    window[base : base + lead, :] = lead_rows[at : at + lead, lanes]
                    window[base + lead : base + span, :] = rows_ref[c, s, :, lanes].astype(F32)
                    value = weight[s, 0:1] * window[base + lead : base + span, :]
                    for j in range(1, staps):
                        value += weight[s, j : j + 1] * window[base + lead - j : base + span - j, :]
                    featured.append(value)
                query_ref[c, :, lanes] = featured[0]
                products.append((featured[1] * featured[2]).astype(BF16))
            picked = pick_own_group(dot(matrix, jnp.concatenate(products, axis=1)), length, per_group)
            for e, c in enumerate(members):
                conv_ref[c, :, lanes] = picked[:, e * LANES : (e + 1) * LANES]


def finish_kernel(peers, cap, dpad, me_ref, owner_ref, decode_owner_ref, query_ref, conv_ref, *rest):
    states, returned = rest[:peers], rest[peers : 2 * peers]
    out_ref, decode_ref, held, places, select = rest[2 * peers :]
    count, length, width = out_ref.shape
    decode_count = decode_owner_ref.shape[0]

    @pl.when(pl.program_id(0) == 0)
    def _():
        for c in range(count):
            places[c] = (owner_ref[c] ^ me_ref[0]) * cap + rank_of(owner_ref, c)
        row = iota((decode_count, 1), 0)
        target = jnp.zeros((decode_count, 1), jnp.int32)
        for n in range(decode_count):
            at = (decode_owner_ref[n] ^ me_ref[0]) * dpad + rank_of(decode_owner_ref, n)
            target = jnp.where(row == n, at, target)
        select[...] = one_hot(iota((decode_count, peers * dpad), 1), target)

    lanes = pl.ds(pl.multiple_of(pl.program_id(0) * width, width), width)
    for k in range(peers):
        for r in range(cap):
            held[k * cap + r] = states[k][r, :, lanes]
    for c in range(count):
        state = held[places[c]].astype(F32)
        out_ref[c] = (query_ref[c, :, lanes] * (conv_ref[c, :, lanes] + state)).astype(BF16)
    arrived = jnp.concatenate([ref[:, lanes].astype(F32) for ref in returned], axis=0).astype(BF16)
    decode_ref[...] = dot(select[...], arrived).astype(BF16)


def per_device(
    stretch_rows,
    stretch_owner,
    send_slot,
    decode_rows,
    row_owner,
    row_slot,
    cache_raw,
    cache_hist,
    short_weight,
    long_filter,
):
    peers = lax.axis_size("ctx")
    cap = send_slot.shape[2]
    count, length, _, channels = stretch_rows.shape
    slots, raw_rows, _, _ = cache_raw.shape
    hist_rows = cache_hist.shape[1]
    staps = short_weight.shape[0]
    groups, taps = long_filter.shape
    per_group = channels // groups
    decode_count = decode_rows.shape[0]
    dcap = max(2, (2 * decode_count + peers - 1) // peers)
    dpad = round_up(dcap, 8)
    planes = 3 * raw_rows
    padded = round_up(planes * cap + 1, 16)
    me = lax.axis_index("ctx").astype(jnp.int32).reshape(1)

    raw2d = cache_raw.transpose(1, 2, 0, 3).reshape(planes * slots, channels)
    hist3d = cache_hist.transpose(1, 0, 2)
    rows2d = decode_rows.transpose(1, 0, 2).reshape(3 * decode_count, channels)
    stretch = stretch_rows.transpose(0, 2, 1, 3)
    weight = short_weight.transpose(1, 0, 2)

    smem = pl.BlockSpec(memory_space=pltpu.SMEM)
    vmem = pl.BlockSpec(memory_space=pltpu.VMEM)
    hbm = pl.BlockSpec(memory_space=pltpu.HBM)
    params = pltpu.CompilerParams(vmem_limit_bytes=32 * 1024 * 1024)

    def tiled(width, *lead):
        return pl.BlockSpec((*lead, width), lambda t: (0,) * len(lead) + (t,))

    def whole(*shape):
        return pl.BlockSpec(shape, lambda t: (0,) * len(shape))

    def cost(flops, data):
        return pl.CostEstimate(flops=1, bytes_accessed=1, transcendentals=0)

    def send(array, k):
        return lax.ppermute(array, "ctx", [(i, i ^ k) for i in range(peers)])

    order = sorted(range(1, peers), reverse=True)
    width = min(512, channels)
    payload = padded + 3 * dpad
    sent = [None] * peers

    def pack(ks, limit, raw_in, rows_in):
        packed = pl.pallas_call(
            functools.partial(pack_kernel, ks, cap, planes, slots, dpad),
            in_specs=[smem] * 4 + [hbm] * 2,
            out_specs=[vmem] * len(ks),
            out_shape=[jax.ShapeDtypeStruct((payload, channels), BF16)] * len(ks),
            scratch_shapes=[
                pltpu.VMEM((planes * slots, channels), BF16),
                pltpu.VMEM((3 * decode_count, channels), BF16),
                pltpu.VMEM((len(ks) * padded, planes * slots), BF16),
                pltpu.VMEM((len(ks), 3 * dpad, 3 * decode_count), BF16),
                pltpu.SemaphoreType.DMA((2,)),
            ],
            compiler_params=pltpu.CompilerParams(vmem_limit_bytes=limit * 1024 * 1024),
            cost_estimate=cost(2 * len(ks) * padded * planes * slots * channels, 4 * planes * slots * channels),
        )(me, send_slot, row_owner, row_slot, raw_in, rows_in)
        for k, block in zip(ks, packed):
            sent[k] = send(block, k) if k else block

    pack(order[:-1], 60, raw2d, rows2d)

    tile_rows = LANES // per_group * length
    history = pl.pallas_call(
        functools.partial(history_kernel, peers, cap, length, per_group),
        grid=(channels // width,),
        in_specs=[smem, smem, whole(groups, taps), tiled(width, hist_rows, slots)],
        out_specs=[tiled(width, cap, length)] * peers + [tiled(width, slots), tiled(width, length)],
        out_shape=[jax.ShapeDtypeStruct((cap, length, channels), BF16)] * peers
        + [jax.ShapeDtypeStruct((slots, channels), F32), jax.ShapeDtypeStruct((length, channels), F32)],
        scratch_shapes=[
            pltpu.VMEM((groups * length, LANES), F32),
            pltpu.VMEM((groups * length, LANES), BF16),
            pltpu.VMEM((groups * length, LANES), BF16),
            pltpu.VMEM((slots, length, width), BF16),
        ],
        compiler_params=pltpu.CompilerParams(vmem_limit_bytes=48 * 1024 * 1024),
        cost_estimate=cost(2 * slots * tile_rows * LANES * channels, 2 * hist_rows * slots * channels),
    )(me, send_slot, long_filter, hist3d)
    states, (first, expanded) = list(history[:peers]), history[peers:]
    raw_in, rows_in, first = lax.optimization_barrier((raw2d, rows2d, first))
    pack([1, 0], 32, raw_in, rows_in)
    for k in order:
        states[k] = send(states[k], k)

    returned = list(
        pl.pallas_call(
            functools.partial(decode_kernel, peers, staps, slots, dpad, planes * cap, padded),
            grid=(channels // width,),
            in_specs=[tiled(width, 3, staps), tiled(width, planes * slots), tiled(width, slots)]
            + [tiled(width, length)]
            + [tiled(width, payload)] * peers
            + [whole(payload, LANES)] * peers,
            out_specs=[tiled(width, dpad)] * peers,
            out_shape=[jax.ShapeDtypeStruct((dpad, channels), BF16)] * peers,
            compiler_params=params,
            cost_estimate=cost(2 * peers * dpad * planes * slots * channels, 4 * planes * slots * channels),
        )(weight, raw2d, first, expanded, *sent, *sent)
    )
    for k in order:
        returned[k] = send(returned[k], k)

    query, conv = pl.pallas_call(
        functools.partial(local_kernel, peers, planes, staps, per_group),
        grid=(channels // width,),
        in_specs=[smem, smem, whole(groups, taps), tiled(width, 3, staps), tiled(width, count, 3, length)]
        + [tiled(width, payload)] * peers,
        out_specs=[tiled(width, count, length)] * 2,
        out_shape=[jax.ShapeDtypeStruct((count, length, channels), F32)] * 2,
        scratch_shapes=[
            pltpu.VMEM((count * 3 * 8, peers * padded), BF16),
            pltpu.VMEM((groups * length, LANES), F32),
            pltpu.VMEM((groups * length, LANES), BF16),
            pltpu.VMEM((2 * count * 3 * (8 + length), LANES), F32),
        ],
        compiler_params=params,
        cost_estimate=cost(2 * count * 24 * peers * padded * channels, 14 * count * length * channels),
    )(me, stretch_owner, long_filter, weight, stretch, *sent)

    return pl.pallas_call(
        functools.partial(finish_kernel, peers, cap, dpad),
        grid=(channels // width,),
        in_specs=[smem, smem, smem] + [vmem] * (2 + 2 * peers),
        out_specs=[tiled(width, count, length), tiled(width, decode_count)],
        out_shape=[
            jax.ShapeDtypeStruct((count, length, channels), BF16),
            jax.ShapeDtypeStruct((decode_count, channels), BF16),
        ],
        scratch_shapes=[
            pltpu.VMEM((peers * cap, length, width), BF16),
            pltpu.SMEM((count,), jnp.int32),
            pltpu.VMEM((decode_count, peers * dpad), BF16),
        ],
        compiler_params=params,
        cost_estimate=cost(3 * count * length * channels, 14 * count * length * channels),
    )(me, stretch_owner, row_owner, query, conv, *states, *returned)


def solution(mesh):
    placed = (
        P(("groups", "ctx"), None, None, "chan"),
        P(("groups", "ctx")),
        P(("groups", "ctx"), None, None),
        P(("groups", "ctx"), None, "chan"),
        P(("groups", "ctx")),
        P(("groups", "ctx")),
        P(("groups", "ctx"), None, None, "chan"),
        P(("groups", "ctx"), None, "chan"),
        P(None, None, "chan"),
        P("chan", None),
    )
    return jax.shard_map(
        per_device,
        mesh=mesh,
        in_specs=placed,
        out_specs=(P(("groups", "ctx"), None, "chan"), P(("groups", "ctx"), "chan")),
        check_vma=False,
    )
```

```python
import functools

import jax
import jax.numpy as jnp
from jax import lax
from jax.experimental import pallas as pl
from jax.experimental.pallas import tpu as pltpu
from jax.sharding import PartitionSpec as P

LANES = 128
F32 = jnp.float32
BF16 = jnp.bfloat16


def round_up(value, unit):
    return (value + unit - 1) // unit * unit


def one_hot(left, right):
    return jnp.where(left == right, 1.0, 0.0).astype(BF16)


def dot(left, right):
    return jnp.dot(left, right, preferred_element_type=F32)


def iota(shape, axis):
    return lax.broadcasted_iota(jnp.int32, shape, axis)


def rank_of(owner_ref, index):
    rank = jnp.int32(0)
    for earlier in range(index):
        rank += (owner_ref[earlier] == owner_ref[index]).astype(jnp.int32)
    return rank


def pick_own_group(stacked, length, per_group):
    lane_group = lax.rem(iota((length, stacked.shape[1]), 1), LANES) // per_group
    picked = stacked[:length]
    for group in range(1, LANES // per_group):
        picked = jnp.where(lane_group == group, stacked[group * length : (group + 1) * length], picked)
    return picked


def pack_kernel(ks, cap, planes, slots, dpad, me_ref, slot_hbm, owner_hbm, code_hbm, raw_hbm, rows_hbm, *rest):
    outs, rest = rest[: len(ks)], rest[len(ks) :]
    slot_ref, owner_ref, code_ref, raw_ref, rows_ref, out_ref, raw_sel, rows_sel, sems = rest
    padded = raw_sel.shape[0] // len(ks)
    decode_count = owner_ref.shape[0]
    channels = raw_ref.shape[1]
    piece = min(512, channels)
    spans = [pl.ds(start, piece) for start in range(0, channels, piece)]
    pairs = [(slot_hbm, slot_ref), (owner_hbm, owner_ref), (code_hbm, code_ref)]
    for lanes in spans:
        pairs += [(raw_hbm.at[:, lanes], raw_ref.at[:, lanes]), (rows_hbm.at[:, lanes], rows_ref.at[:, lanes])]
    copies = [pltpu.make_async_copy(source, target, sems.at[at]) for at, (source, target) in enumerate(pairs)]
    for copy in copies:
        copy.start()
    for copy in copies[:3]:
        copy.wait()

    row = iota((padded, 1), 0)
    column = iota((padded, planes * slots), 1)
    lane = iota((1, 3 * decode_count), 1)
    wide = iota((1, LANES), 1)
    codes, places = [], []
    for at, k in enumerate(ks):
        peer = me_ref[0] ^ k
        target = jnp.full((padded, 1), -1, jnp.int32)
        for r in range(cap):
            slot = jnp.maximum(slot_ref[0, peer, r], 0)
            here = (row >= r * planes) & (row < (r + 1) * planes)
            target = jnp.where(here, (row - r * planes) * slots + slot, target)
        raw_sel[at * padded : (at + 1) * padded, :] = one_hot(column, target)
        target = jnp.full((1, 3 * decode_count), -1, jnp.int32)
        code = jnp.full((1, LANES), -1, jnp.int32)
        rank = jnp.int32(0)
        for n in range(decode_count):
            mine = owner_ref[n] == peer
            for s in range(3):
                hit = jnp.where(mine, s * decode_count + n, -1)
                target = jnp.where(lane == hit, rank + s * dpad, target)
            code = jnp.where(wide == jnp.where(mine, rank, -1), code_ref[n], code)
            rank += mine.astype(jnp.int32)
        places.append(one_hot(iota((3 * dpad, 3 * decode_count), 0), target).astype(F32))
        codes.append(code.astype(F32))

    rows_sel[...] = jnp.concatenate(places, axis=0).astype(BF16)
    marked = iota((padded, LANES), 0) == cap * planes
    leaving = []
    for step, lanes in enumerate(spans):
        copies[3 + 2 * step].wait()
        copies[4 + 2 * step].wait()
        picked = dot(raw_sel[...], raw_ref[:, lanes])
        placed = dot(rows_sel[...], rows_ref[:, lanes])
        for at in range(len(ks)):
            raw = picked[at * padded : (at + 1) * padded]
            if step == 0:
                head = jnp.where(marked, codes[at], raw[:, :LANES])
                raw = jnp.concatenate([head, raw[:, LANES:]], axis=1)
            rows = placed[at * 3 * dpad : (at + 1) * 3 * dpad]
            out_ref[at, :, lanes] = jnp.concatenate([raw, rows], axis=0).astype(BF16)
            sem = sems.at[len(copies) + len(leaving)]
            leaving.append(pltpu.make_async_copy(out_ref.at[at, :, lanes], outs[at].at[:, lanes], sem))
            leaving[-1].start()
    for copy in leaving:
        copy.wait()


def history_kernel(peers, cap, length, per_group, me_ref, slot_ref, filter_ref, hist_ref, *rest):
    sends, (first_ref, taps_ref) = rest[:peers], rest[peers : peers + 2]
    stage, toeplitz, local, states = rest[peers + 2 :]
    hist_rows, slots, _ = hist_ref.shape
    groups, taps = filter_ref.shape
    tile_rows = LANES // per_group * length

    @pl.when(pl.program_id(0) == 0)
    def _():
        source, column = iota((taps, LANES), 0), iota((taps, LANES), 1)
        for i in range(length):
            shift = jnp.where(column < hist_rows, one_hot(source, taps - 1 + i - column).astype(F32), 0.0)
            stage[pl.ds(i, groups, stride=length), :] = dot(filter_ref[...], shift.astype(BF16))
        toeplitz[...] = stage[: groups * length, :].astype(BF16)
        for i in range(length):
            stage[pl.ds(i, groups, stride=length), :] = dot(filter_ref[...], one_hot(source, i - column))
        local[...] = stage[: groups * length, :].astype(BF16)

    column0 = jnp.where(iota((LANES, LANES), 0) == 0, 1.0, 0.0).astype(BF16)
    tiles = hist_ref.shape[2] // LANES
    for tile in range(tiles):
        start = pl.multiple_of((pl.program_id(0) * tiles + tile) * tile_rows, tile_rows)
        lanes = slice(tile * LANES, (tile + 1) * LANES)
        expanded = dot(local[pl.ds(start, tile_rows), :], column0)
        taps_ref[:, lanes] = pick_own_group(expanded, length, per_group)
        matrix = toeplitz[pl.ds(start, tile_rows), :]
        block = hist_ref[:, :, lanes]
        rest_rows = jnp.zeros((LANES - hist_rows, slots, LANES), BF16)
        by_slot = jnp.swapaxes(jnp.concatenate([block, rest_rows], axis=0), 0, 1)
        for slot in range(0, slots, 2):
            pair = jnp.concatenate([by_slot[slot], by_slot[slot + 1]], axis=1)
            picked = pick_own_group(dot(matrix, pair), length, per_group)
            for e in range(2):
                own = picked[:, e * LANES : (e + 1) * LANES]
                states[slot + e, :, lanes] = own.astype(BF16)
                first_ref[slot + e : slot + e + 1, lanes] = own[:1]
    for k in range(peers):
        for r in range(cap):
            sends[k][r] = states[jnp.maximum(slot_ref[0, me_ref[0] ^ k, r], 0)]


def decode_kernel(peers, staps, slots, dpad, mark, padded, weight_ref, raw_ref, first_ref, taps_ref, *rest):
    rows, codes, outs = rest[:peers], rest[peers : 2 * peers], rest[2 * peers :]
    lane = iota((slots, LANES), 0)
    selects = []
    for ref in codes:
        code = ref[...].astype(F32)[mark : mark + 1].astype(jnp.int32)
        selects.append(jnp.where(lane == code, 1.0, 0.0).T[:dpad])
    select = jnp.concatenate(selects, axis=0)
    arrived = [ref[...].astype(F32)[padded:] for ref in rows]
    weight = weight_ref[...].astype(F32)
    featured = []
    for s in range(3):
        own = jnp.concatenate([block[s * dpad : (s + 1) * dpad] for block in arrived], axis=0)
        value = weight[s, 0:1] * own
        for j in range(1, staps):
            plane = (staps - 1 - j) * 3 + s
            state = dot(select.astype(BF16), raw_ref[plane * slots : (plane + 1) * slots, :])
            value += weight[s, j : j + 1] * state
        featured.append(value)
    gated = (featured[1] * featured[2]).astype(BF16).astype(F32)
    history = jnp.dot(select, first_ref[...], preferred_element_type=F32, precision=lax.Precision.HIGHEST)
    result = featured[0] * (taps_ref[0:1, :] * gated + history)
    for k in range(peers):
        outs[k][...] = result[k * dpad : (k + 1) * dpad].astype(BF16)


def local_kernel(peers, planes, staps, per_group, me_ref, owner_ref, filter_ref, weight_ref, rows_ref, *rest):
    raws, (query_ref, conv_ref) = rest[:peers], rest[peers : peers + 2]
    select, stage, local, window = rest[peers + 2 :]
    count, _, length, _ = rows_ref.shape
    groups, taps = filter_ref.shape
    padded = select.shape[1] // peers
    tile_rows = LANES // per_group * length
    lead = 8
    span = lead + length

    @pl.when(pl.program_id(0) == 0)
    def _():
        source, column = iota((taps, LANES), 0), iota((taps, LANES), 1)
        for i in range(length):
            stage[pl.ds(i, groups, stride=length), :] = dot(filter_ref[...], one_hot(source, i - column))
        local[...] = stage[...].astype(BF16)
        row = iota((lead, 1), 0) - (lead - staps + 1)
        targets = []
        for c in range(count):
            base = (owner_ref[c] ^ me_ref[0]) * padded + rank_of(owner_ref, c) * planes
            targets += [jnp.where(row >= 0, base + row * 3 + s, -1) for s in range(3)]
        select[...] = one_hot(iota(select.shape, 1), jnp.concatenate(targets, axis=0))

    lead_rows = dot(select[...], jnp.concatenate([ref[...][:padded] for ref in raws], axis=0))
    weights = weight_ref[...].astype(F32)
    tiles = rows_ref.shape[3] // LANES
    for tile in range(tiles):
        start = pl.multiple_of((pl.program_id(0) * tiles + tile) * tile_rows, tile_rows)
        lanes = slice(tile * LANES, (tile + 1) * LANES)
        matrix = local[pl.ds(start, tile_rows), :][:, :length]
        weight = weights[:, :, lanes]
        for first in range(0, count, 2):
            members = range(first, min(first + 2, count))
            products = []
            for c in members:
                featured = []
                for s in range(3):
                    base = (((tile % 2) * count + c) * 3 + s) * span
                    at = (c * 3 + s) * lead
                    window[base : base + lead, :] = lead_rows[at : at + lead, lanes]
                    window[base + lead : base + span, :] = rows_ref[c, s, :, lanes].astype(F32)
                    value = weight[s, 0:1] * window[base + lead : base + span, :]
                    for j in range(1, staps):
                        value += weight[s, j : j + 1] * window[base + lead - j : base + span - j, :]
                    featured.append(value)
                query_ref[c, :, lanes] = featured[0]
                products.append((featured[1] * featured[2]).astype(BF16))
            picked = pick_own_group(dot(matrix, jnp.concatenate(products, axis=1)), length, per_group)
            for e, c in enumerate(members):
                conv_ref[c, :, lanes] = picked[:, e * LANES : (e + 1) * LANES]


def finish_kernel(peers, cap, dpad, me_ref, owner_ref, decode_owner_ref, query_ref, conv_ref, *rest):
    states, returned = rest[:peers], rest[peers : 2 * peers]
    out_ref, decode_ref, held, places, select = rest[2 * peers :]
    count, length, width = out_ref.shape
    decode_count = decode_owner_ref.shape[0]

    @pl.when(pl.program_id(0) == 0)
    def _():
        for c in range(count):
            places[c] = (owner_ref[c] ^ me_ref[0]) * cap + rank_of(owner_ref, c)
        row = iota((decode_count, 1), 0)
        target = jnp.zeros((decode_count, 1), jnp.int32)
        for n in range(decode_count):
            at = (decode_owner_ref[n] ^ me_ref[0]) * dpad + rank_of(decode_owner_ref, n)
            target = jnp.where(row == n, at, target)
        select[...] = one_hot(iota((decode_count, peers * dpad), 1), target)

    lanes = pl.ds(pl.multiple_of(pl.program_id(0) * width, width), width)
    for k in range(peers):
        for r in range(cap):
            held[k * cap + r] = states[k][r, :, lanes]
    for c in range(count):
        state = held[places[c]].astype(F32)
        out_ref[c] = (query_ref[c, :, lanes] * (conv_ref[c, :, lanes] + state)).astype(BF16)
    arrived = jnp.concatenate([ref[:, lanes].astype(F32) for ref in returned], axis=0).astype(BF16)
    decode_ref[...] = dot(select[...], arrived).astype(BF16)


def per_device(
    stretch_rows,
    stretch_owner,
    send_slot,
    decode_rows,
    row_owner,
    row_slot,
    cache_raw,
    cache_hist,
    short_weight,
    long_filter,
):
    peers = lax.axis_size("ctx")
    cap = send_slot.shape[2]
    count, length, _, channels = stretch_rows.shape
    slots, raw_rows, _, _ = cache_raw.shape
    hist_rows = cache_hist.shape[1]
    staps = short_weight.shape[0]
    groups, taps = long_filter.shape
    per_group = channels // groups
    decode_count = decode_rows.shape[0]
    dcap = max(2, (2 * decode_count + peers - 1) // peers)
    dpad = round_up(dcap, 8)
    planes = 3 * raw_rows
    padded = round_up(planes * cap + 1, 16)
    me = lax.axis_index("ctx").astype(jnp.int32).reshape(1)

    raw2d = cache_raw.transpose(1, 2, 0, 3).reshape(planes * slots, channels)
    hist3d = cache_hist.transpose(1, 0, 2)
    rows2d = decode_rows.transpose(1, 0, 2).reshape(3 * decode_count, channels)
    stretch = stretch_rows.transpose(0, 2, 1, 3)
    weight = short_weight.transpose(1, 0, 2)

    smem = pl.BlockSpec(memory_space=pltpu.SMEM)
    vmem = pl.BlockSpec(memory_space=pltpu.VMEM)
    hbm = pl.BlockSpec(memory_space=pltpu.HBM)
    params = pltpu.CompilerParams(vmem_limit_bytes=32 * 1024 * 1024)

    def tiled(width, *lead):
        return pl.BlockSpec((*lead, width), lambda t: (0,) * len(lead) + (t,))

    def whole(*shape):
        return pl.BlockSpec(shape, lambda t: (0,) * len(shape))

    def cost(flops, data):
        return pl.CostEstimate(flops=1, bytes_accessed=1, transcendentals=0)

    def send(array, k):
        return lax.ppermute(array, "ctx", [(i, i ^ k) for i in range(peers)])

    order = sorted(range(1, peers), reverse=True)
    width = min(512, channels)
    payload = padded + 3 * dpad
    sent = [None] * peers

    def pack(ks, limit, raw_in, rows_in):
        packed = pl.pallas_call(
            functools.partial(pack_kernel, ks, cap, planes, slots, dpad),
            in_specs=[smem] + [hbm] * 5,
            out_specs=[hbm] * len(ks),
            out_shape=[jax.ShapeDtypeStruct((payload, channels), BF16)] * len(ks),
            scratch_shapes=[
                pltpu.SMEM(send_slot.shape, jnp.int32),
                pltpu.SMEM(row_owner.shape, jnp.int32),
                pltpu.SMEM(row_slot.shape, jnp.int32),
                pltpu.VMEM((planes * slots, channels), BF16),
                pltpu.VMEM((3 * decode_count, channels), BF16),
                pltpu.VMEM((len(ks), payload, channels), BF16),
                pltpu.VMEM((len(ks) * padded, planes * slots), BF16),
                pltpu.VMEM((len(ks) * 3 * dpad, 3 * decode_count), BF16),
                pltpu.SemaphoreType.DMA((3 + (2 + len(ks)) * -(-channels // 512),)),
            ],
            compiler_params=pltpu.CompilerParams(vmem_limit_bytes=limit * 1024 * 1024),
            cost_estimate=cost(2 * len(ks) * padded * planes * slots * channels, 4 * planes * slots * channels),
        )(me, send_slot, row_owner, row_slot, raw_in, rows_in)
        for k, block in zip(ks, packed):
            sent[k] = send(block, k) if k else block

    pack(order[:-1], 60, raw2d, rows2d)

    tile_rows = LANES // per_group * length
    history = pl.pallas_call(
        functools.partial(history_kernel, peers, cap, length, per_group),
        grid=(channels // width,),
        in_specs=[smem, smem, whole(groups, taps), tiled(width, hist_rows, slots)],
        out_specs=[tiled(width, cap, length)] * peers + [tiled(width, slots), tiled(width, length)],
        out_shape=[jax.ShapeDtypeStruct((cap, length, channels), BF16)] * peers
        + [jax.ShapeDtypeStruct((slots, channels), F32), jax.ShapeDtypeStruct((length, channels), F32)],
        scratch_shapes=[
            pltpu.VMEM((groups * length, LANES), F32),
            pltpu.VMEM((groups * length, LANES), BF16),
            pltpu.VMEM((groups * length, LANES), BF16),
            pltpu.VMEM((slots, length, width), BF16),
        ],
        compiler_params=pltpu.CompilerParams(vmem_limit_bytes=48 * 1024 * 1024),
        cost_estimate=cost(2 * slots * tile_rows * LANES * channels, 2 * hist_rows * slots * channels),
    )(me, send_slot, long_filter, hist3d)
    states, (first, expanded) = list(history[:peers]), history[peers:]
    raw_in, rows_in, first = lax.optimization_barrier((raw2d, rows2d, first))
    pack([1, 0], 32, raw_in, rows_in)
    for k in order:
        states[k] = send(states[k], k)

    returned = list(
        pl.pallas_call(
            functools.partial(decode_kernel, peers, staps, slots, dpad, planes * cap, padded),
            grid=(channels // width,),
            in_specs=[tiled(width, 3, staps), tiled(width, planes * slots), tiled(width, slots)]
            + [tiled(width, length)]
            + [tiled(width, payload)] * peers
            + [whole(payload, LANES)] * peers,
            out_specs=[tiled(width, dpad)] * peers,
            out_shape=[jax.ShapeDtypeStruct((dpad, channels), BF16)] * peers,
            compiler_params=params,
            cost_estimate=cost(2 * peers * dpad * planes * slots * channels, 4 * planes * slots * channels),
        )(weight, raw2d, first, expanded, *sent, *sent)
    )
    for k in order:
        returned[k] = send(returned[k], k)

    query, conv = pl.pallas_call(
        functools.partial(local_kernel, peers, planes, staps, per_group),
        grid=(channels // width,),
        in_specs=[smem, smem, whole(groups, taps), tiled(width, 3, staps), tiled(width, count, 3, length)]
        + [tiled(width, payload)] * peers,
        out_specs=[tiled(width, count, length)] * 2,
        out_shape=[jax.ShapeDtypeStruct((count, length, channels), F32)] * 2,
        scratch_shapes=[
            pltpu.VMEM((count * 3 * 8, peers * padded), BF16),
            pltpu.VMEM((groups * length, LANES), F32),
            pltpu.VMEM((groups * length, LANES), BF16),
            pltpu.VMEM((2 * count * 3 * (8 + length), LANES), F32),
        ],
        compiler_params=params,
        cost_estimate=cost(2 * count * 24 * peers * padded * channels, 14 * count * length * channels),
    )(me, stretch_owner, long_filter, weight, stretch, *sent)

    wide = min(1024, channels)
    return pl.pallas_call(
        functools.partial(finish_kernel, peers, cap, dpad),
        grid=(channels // wide,),
        in_specs=[smem, smem, smem] + [vmem] * (2 + 2 * peers),
        out_specs=[tiled(wide, count, length), tiled(wide, decode_count)],
        out_shape=[
            jax.ShapeDtypeStruct((count, length, channels), BF16),
            jax.ShapeDtypeStruct((decode_count, channels), BF16),
        ],
        scratch_shapes=[
            pltpu.VMEM((peers * cap, length, wide), BF16),
            pltpu.SMEM((count,), jnp.int32),
            pltpu.VMEM((decode_count, peers * dpad), BF16),
        ],
        compiler_params=params,
        cost_estimate=cost(3 * count * length * channels, 14 * count * length * channels),
    )(me, stretch_owner, row_owner, query, conv, *states, *returned)


def solution(mesh):
    placed = (
        P(("groups", "ctx"), None, None, "chan"),
        P(("groups", "ctx")),
        P(("groups", "ctx"), None, None),
        P(("groups", "ctx"), None, "chan"),
        P(("groups", "ctx")),
        P(("groups", "ctx")),
        P(("groups", "ctx"), None, None, "chan"),
        P(("groups", "ctx"), None, "chan"),
        P(None, None, "chan"),
        P("chan", None),
    )
    return jax.shard_map(
        per_device,
        mesh=mesh,
        in_specs=placed,
        out_specs=(P(("groups", "ctx"), None, "chan"), P(("groups", "ctx"), "chan")),
        check_vma=False,
    )
```

```python
import functools

import jax
import jax.numpy as jnp
from jax import lax
from jax.experimental import pallas as pl
from jax.experimental.pallas import tpu as pltpu
from jax.sharding import PartitionSpec as P

LANES = 128
F32 = jnp.float32
BF16 = jnp.bfloat16


def round_up(value, unit):
    return (value + unit - 1) // unit * unit


def one_hot(left, right):
    return jnp.where(left == right, 1.0, 0.0).astype(BF16)


def dot(left, right):
    return jnp.dot(left, right, preferred_element_type=F32)


def iota(shape, axis):
    return lax.broadcasted_iota(jnp.int32, shape, axis)


def rank_of(owner_ref, index):
    rank = jnp.int32(0)
    for earlier in range(index):
        rank += (owner_ref[earlier] == owner_ref[index]).astype(jnp.int32)
    return rank


def pick_own_group(stacked, length, per_group):
    lane_group = lax.rem(iota((length, stacked.shape[1]), 1), LANES) // per_group
    picked = stacked[:length]
    for group in range(1, LANES // per_group):
        picked = jnp.where(lane_group == group, stacked[group * length : (group + 1) * length], picked)
    return picked


def pack_kernel(ks, cap, planes, slots, dpad, me_ref, slot_hbm, owner_hbm, code_hbm, raw_hbm, rows_hbm, *rest):
    outs, rest = rest[: len(ks)], rest[len(ks) :]
    slot_ref, owner_ref, code_ref, raw_ref, rows_ref, out_ref, raw_sel, rows_sel, sems = rest
    padded = raw_sel.shape[0] // len(ks)
    decode_count = owner_ref.shape[0]
    channels = raw_ref.shape[1]
    piece = min(512, channels)
    spans = [pl.ds(start, piece) for start in range(0, channels, piece)]
    pairs = [(slot_hbm, slot_ref), (owner_hbm, owner_ref), (code_hbm, code_ref)]
    for lanes in spans:
        pairs += [(raw_hbm.at[:, lanes], raw_ref.at[:, lanes]), (rows_hbm.at[:, lanes], rows_ref.at[:, lanes])]
    copies = [pltpu.make_async_copy(source, target, sems.at[at]) for at, (source, target) in enumerate(pairs)]
    for copy in copies:
        copy.start()
    for copy in copies[:3]:
        copy.wait()

    row = iota((padded, 1), 0)
    column = iota((padded, planes * slots), 1)
    lane = iota((1, 3 * decode_count), 1)
    wide = iota((1, LANES), 1)
    codes, places = [], []
    for at, k in enumerate(ks):
        peer = me_ref[0] ^ k
        target = jnp.full((padded, 1), -1, jnp.int32)
        for r in range(cap):
            slot = jnp.maximum(slot_ref[0, peer, r], 0)
            here = (row >= r * planes) & (row < (r + 1) * planes)
            target = jnp.where(here, (row - r * planes) * slots + slot, target)
        raw_sel[at * padded : (at + 1) * padded, :] = one_hot(column, target)
        target = jnp.full((1, 3 * decode_count), -1, jnp.int32)
        code = jnp.full((1, LANES), -1, jnp.int32)
        rank = jnp.int32(0)
        for n in range(decode_count):
            mine = owner_ref[n] == peer
            for s in range(3):
                hit = jnp.where(mine, s * decode_count + n, -1)
                target = jnp.where(lane == hit, rank + s * dpad, target)
            code = jnp.where(wide == jnp.where(mine, rank, -1), code_ref[n], code)
            rank += mine.astype(jnp.int32)
        places.append(one_hot(iota((3 * dpad, 3 * decode_count), 0), target).astype(F32))
        codes.append(code.astype(F32))

    rows_sel[...] = jnp.concatenate(places, axis=0).astype(BF16)
    marked = iota((padded, LANES), 0) == cap * planes
    leaving = []
    for step, lanes in enumerate(spans):
        copies[3 + 2 * step].wait()
        copies[4 + 2 * step].wait()
        picked = dot(raw_sel[...], raw_ref[:, lanes])
        placed = dot(rows_sel[...], rows_ref[:, lanes])
        for at in range(len(ks)):
            raw = picked[at * padded : (at + 1) * padded]
            if step == 0:
                head = jnp.where(marked, codes[at], raw[:, :LANES])
                raw = jnp.concatenate([head, raw[:, LANES:]], axis=1)
            rows = placed[at * 3 * dpad : (at + 1) * 3 * dpad]
            out_ref[at, :, lanes] = jnp.concatenate([raw, rows], axis=0).astype(BF16)
            sem = sems.at[len(copies) + len(leaving)]
            leaving.append(pltpu.make_async_copy(out_ref.at[at, :, lanes], outs[at].at[:, lanes], sem))
            leaving[-1].start()
    for copy in leaving:
        copy.wait()


def history_kernel(peers, cap, length, per_group, me_ref, slot_ref, filter_ref, hist_ref, *rest):
    sends, (first_ref, taps_ref) = rest[:peers], rest[peers : peers + 2]
    stage, toeplitz, local, states = rest[peers + 2 :]
    hist_rows, slots, _ = hist_ref.shape
    groups, taps = filter_ref.shape
    tile_rows = LANES // per_group * length

    @pl.when(pl.program_id(0) == 0)
    def _():
        source, column = iota((taps, LANES), 0), iota((taps, LANES), 1)
        for i in range(length):
            shift = jnp.where(column < hist_rows, one_hot(source, taps - 1 + i - column).astype(F32), 0.0)
            stage[pl.ds(i, groups, stride=length), :] = dot(filter_ref[...], shift.astype(BF16))
        toeplitz[...] = stage[: groups * length, :].astype(BF16)
        for i in range(length):
            stage[pl.ds(i, groups, stride=length), :] = dot(filter_ref[...], one_hot(source, i - column))
        local[...] = stage[: groups * length, :].astype(BF16)

    column0 = jnp.where(iota((LANES, LANES), 0) == 0, 1.0, 0.0).astype(BF16)
    tiles = hist_ref.shape[2] // LANES
    for tile in range(tiles):
        start = pl.multiple_of((pl.program_id(0) * tiles + tile) * tile_rows, tile_rows)
        lanes = slice(tile * LANES, (tile + 1) * LANES)
        expanded = dot(local[pl.ds(start, tile_rows), :], column0)
        taps_ref[:, lanes] = pick_own_group(expanded, length, per_group)
        matrix = toeplitz[pl.ds(start, tile_rows), :]
        block = hist_ref[:, :, lanes]
        rest_rows = jnp.zeros((LANES - hist_rows, slots, LANES), BF16)
        by_slot = jnp.swapaxes(jnp.concatenate([block, rest_rows], axis=0), 0, 1)
        for slot in range(0, slots, 2):
            pair = jnp.concatenate([by_slot[slot], by_slot[slot + 1]], axis=1)
            picked = pick_own_group(dot(matrix, pair), length, per_group)
            for e in range(2):
                own = picked[:, e * LANES : (e + 1) * LANES]
                states[slot + e, :, lanes] = own.astype(BF16)
                first_ref[slot + e : slot + e + 1, lanes] = own[:1]
    for k in range(peers):
        for r in range(cap):
            sends[k][r] = states[jnp.maximum(slot_ref[0, me_ref[0] ^ k, r], 0)]


def decode_kernel(peers, staps, slots, dpad, mark, padded, weight_ref, raw_ref, first_ref, taps_ref, *rest):
    rows, codes, outs = rest[:peers], rest[peers : 2 * peers], rest[2 * peers :]
    lane = iota((slots, LANES), 0)
    selects = []
    for ref in codes:
        code = ref[...].astype(F32)[mark : mark + 1].astype(jnp.int32)
        selects.append(jnp.where(lane == code, 1.0, 0.0).T[:dpad])
    select = jnp.concatenate(selects, axis=0)
    arrived = [ref[...].astype(F32)[padded:] for ref in rows]
    weight = weight_ref[...].astype(F32)
    featured = []
    for s in range(3):
        own = jnp.concatenate([block[s * dpad : (s + 1) * dpad] for block in arrived], axis=0)
        value = weight[s, 0:1] * own
        for j in range(1, staps):
            plane = (staps - 1 - j) * 3 + s
            state = dot(select.astype(BF16), raw_ref[plane * slots : (plane + 1) * slots, :])
            value += weight[s, j : j + 1] * state
        featured.append(value)
    gated = (featured[1] * featured[2]).astype(BF16).astype(F32)
    history = jnp.dot(select, first_ref[...], preferred_element_type=F32, precision=lax.Precision.HIGHEST)
    result = featured[0] * (taps_ref[0:1, :] * gated + history)
    for k in range(peers):
        outs[k][...] = result[k * dpad : (k + 1) * dpad].astype(BF16)


def local_kernel(peers, planes, staps, per_group, me_ref, owner_ref, filter_ref, weight_ref, rows_ref, *rest):
    raws, (query_ref, conv_ref) = rest[:peers], rest[peers : peers + 2]
    select, stage, local, window = rest[peers + 2 :]
    count, _, length, _ = rows_ref.shape
    groups, taps = filter_ref.shape
    padded = select.shape[1] // peers
    tile_rows = LANES // per_group * length
    lead = 8
    span = lead + length

    @pl.when(pl.program_id(0) == 0)
    def _():
        source, column = iota((taps, LANES), 0), iota((taps, LANES), 1)
        for i in range(length):
            stage[pl.ds(i, groups, stride=length), :] = dot(filter_ref[...], one_hot(source, i - column))
        local[...] = stage[...].astype(BF16)
        row = iota((lead, 1), 0) - (lead - staps + 1)
        targets = []
        for c in range(count):
            base = (owner_ref[c] ^ me_ref[0]) * padded + rank_of(owner_ref, c) * planes
            targets += [jnp.where(row >= 0, base + row * 3 + s, -1) for s in range(3)]
        select[...] = one_hot(iota(select.shape, 1), jnp.concatenate(targets, axis=0))

    lead_rows = dot(select[...], jnp.concatenate([ref[...][:padded] for ref in raws], axis=0))
    weights = weight_ref[...].astype(F32)
    tiles = rows_ref.shape[3] // LANES
    for tile in range(tiles):
        start = pl.multiple_of((pl.program_id(0) * tiles + tile) * tile_rows, tile_rows)
        lanes = slice(tile * LANES, (tile + 1) * LANES)
        matrix = local[pl.ds(start, tile_rows), :][:, :length]
        weight = weights[:, :, lanes]
        for first in range(0, count, 2):
            members = range(first, min(first + 2, count))
            products = []
            for c in members:
                featured = []
                for s in range(3):
                    base = (((tile % 2) * count + c) * 3 + s) * span
                    at = (c * 3 + s) * lead
                    window[base : base + lead, :] = lead_rows[at : at + lead, lanes]
                    window[base + lead : base + span, :] = rows_ref[c, s, :, lanes].astype(F32)
                    value = weight[s, 0:1] * window[base + lead : base + span, :]
                    for j in range(1, staps):
                        value += weight[s, j : j + 1] * window[base + lead - j : base + span - j, :]
                    featured.append(value)
                query_ref[c, :, lanes] = featured[0]
                products.append((featured[1] * featured[2]).astype(BF16))
            picked = pick_own_group(dot(matrix, jnp.concatenate(products, axis=1)), length, per_group)
            for e, c in enumerate(members):
                conv_ref[c, :, lanes] = picked[:, e * LANES : (e + 1) * LANES]


def finish_kernel(peers, cap, dpad, me_ref, owner_ref, decode_owner_ref, query_ref, conv_ref, *rest):
    states, returned = rest[:peers], rest[peers : 2 * peers]
    out_ref, decode_ref, held, places, select = rest[2 * peers :]
    count, length, width = out_ref.shape
    decode_count = decode_owner_ref.shape[0]

    @pl.when(pl.program_id(0) == 0)
    def _():
        for c in range(count):
            places[c] = (owner_ref[c] ^ me_ref[0]) * cap + rank_of(owner_ref, c)
        row = iota((decode_count, 1), 0)
        target = jnp.zeros((decode_count, 1), jnp.int32)
        for n in range(decode_count):
            at = (decode_owner_ref[n] ^ me_ref[0]) * dpad + rank_of(decode_owner_ref, n)
            target = jnp.where(row == n, at, target)
        select[...] = one_hot(iota((decode_count, peers * dpad), 1), target)

    lanes = pl.ds(pl.multiple_of(pl.program_id(0) * width, width), width)
    for k in range(peers):
        for r in range(cap):
            held[k * cap + r] = states[k][r, :, lanes]
    for c in range(count):
        state = held[places[c]].astype(F32)
        out_ref[c] = (query_ref[c, :, lanes] * (conv_ref[c, :, lanes] + state)).astype(BF16)
    arrived = jnp.concatenate([ref[:, lanes].astype(F32) for ref in returned], axis=0).astype(BF16)
    decode_ref[...] = dot(select[...], arrived).astype(BF16)


def per_device(
    stretch_rows,
    stretch_owner,
    send_slot,
    decode_rows,
    row_owner,
    row_slot,
    cache_raw,
    cache_hist,
    short_weight,
    long_filter,
):
    peers = lax.axis_size("ctx")
    cap = send_slot.shape[2]
    count, length, _, channels = stretch_rows.shape
    slots, raw_rows, _, _ = cache_raw.shape
    hist_rows = cache_hist.shape[1]
    staps = short_weight.shape[0]
    groups, taps = long_filter.shape
    per_group = channels // groups
    decode_count = decode_rows.shape[0]
    dcap = max(2, (2 * decode_count + peers - 1) // peers)
    dpad = round_up(dcap, 8)
    planes = 3 * raw_rows
    padded = round_up(planes * cap + 1, 16)
    me = lax.axis_index("ctx").astype(jnp.int32).reshape(1)

    raw2d = cache_raw.transpose(1, 2, 0, 3).reshape(planes * slots, channels)
    hist3d = cache_hist.transpose(1, 0, 2)
    rows2d = decode_rows.transpose(1, 0, 2).reshape(3 * decode_count, channels)
    stretch = stretch_rows.transpose(0, 2, 1, 3)
    weight = short_weight.transpose(1, 0, 2)

    smem = pl.BlockSpec(memory_space=pltpu.SMEM)
    vmem = pl.BlockSpec(memory_space=pltpu.VMEM)
    hbm = pl.BlockSpec(memory_space=pltpu.HBM)
    params = pltpu.CompilerParams(vmem_limit_bytes=24 * 1024 * 1024)

    def tiled(width, *lead):
        return pl.BlockSpec((*lead, width), lambda t: (0,) * len(lead) + (t,))

    def whole(*shape):
        return pl.BlockSpec(shape, lambda t: (0,) * len(shape))

    def cost(flops, data):
        return pl.CostEstimate(flops=1, bytes_accessed=1, transcendentals=0)

    def send(array, k):
        return lax.ppermute(array, "ctx", [(i, i ^ k) for i in range(peers)])

    order = sorted(range(1, peers), reverse=True)
    width = min(512, channels)
    payload = padded + 3 * dpad
    sent = [None] * peers

    def pack(ks, limit, raw_in, rows_in):
        packed = pl.pallas_call(
            functools.partial(pack_kernel, ks, cap, planes, slots, dpad),
            in_specs=[smem] + [hbm] * 5,
            out_specs=[hbm] * len(ks),
            out_shape=[jax.ShapeDtypeStruct((payload, channels), BF16)] * len(ks),
            scratch_shapes=[
                pltpu.SMEM(send_slot.shape, jnp.int32),
                pltpu.SMEM(row_owner.shape, jnp.int32),
                pltpu.SMEM(row_slot.shape, jnp.int32),
                pltpu.VMEM((planes * slots, channels), BF16),
                pltpu.VMEM((3 * decode_count, channels), BF16),
                pltpu.VMEM((len(ks), payload, channels), BF16),
                pltpu.VMEM((len(ks) * padded, planes * slots), BF16),
                pltpu.VMEM((len(ks) * 3 * dpad, 3 * decode_count), BF16),
                pltpu.SemaphoreType.DMA((3 + (2 + len(ks)) * -(-channels // 512),)),
            ],
            compiler_params=pltpu.CompilerParams(vmem_limit_bytes=limit * 1024 * 1024),
            cost_estimate=cost(2 * len(ks) * padded * planes * slots * channels, 4 * planes * slots * channels),
        )(me, send_slot, row_owner, row_slot, raw_in, rows_in)
        for k, block in zip(ks, packed):
            sent[k] = send(block, k) if k else block

    pack(order[:-1], 60, raw2d, rows2d)

    tile_rows = LANES // per_group * length
    history = pl.pallas_call(
        functools.partial(history_kernel, peers, cap, length, per_group),
        grid=(channels // width,),
        in_specs=[smem, smem, whole(groups, taps), tiled(width, hist_rows, slots)],
        out_specs=[tiled(width, cap, length)] * peers + [tiled(width, slots), tiled(width, length)],
        out_shape=[jax.ShapeDtypeStruct((cap, length, channels), BF16)] * peers
        + [jax.ShapeDtypeStruct((slots, channels), F32), jax.ShapeDtypeStruct((length, channels), F32)],
        scratch_shapes=[
            pltpu.VMEM((groups * length, LANES), F32),
            pltpu.VMEM((groups * length, LANES), BF16),
            pltpu.VMEM((groups * length, LANES), BF16),
            pltpu.VMEM((slots, length, width), BF16),
        ],
        compiler_params=pltpu.CompilerParams(vmem_limit_bytes=48 * 1024 * 1024),
        cost_estimate=cost(2 * slots * tile_rows * LANES * channels, 2 * hist_rows * slots * channels),
    )(me, send_slot, long_filter, hist3d)
    states, (first, expanded) = list(history[:peers]), history[peers:]
    raw_in, rows_in, first = lax.optimization_barrier((raw2d, rows2d, first))
    pack([1, 0], 32, raw_in, rows_in)
    for k in order:
        states[k] = send(states[k], k)

    returned = list(
        pl.pallas_call(
            functools.partial(decode_kernel, peers, staps, slots, dpad, planes * cap, padded),
            grid=(channels // width,),
            in_specs=[tiled(width, 3, staps), tiled(width, planes * slots), tiled(width, slots)]
            + [tiled(width, length)]
            + [tiled(width, payload)] * peers
            + [whole(payload, LANES)] * peers,
            out_specs=[tiled(width, dpad)] * peers,
            out_shape=[jax.ShapeDtypeStruct((dpad, channels), BF16)] * peers,
            compiler_params=params,
            cost_estimate=cost(2 * peers * dpad * planes * slots * channels, 4 * planes * slots * channels),
        )(weight, raw2d, first, expanded, *sent, *sent)
    )
    for k in order:
        returned[k] = send(returned[k], k)

    query, conv = pl.pallas_call(
        functools.partial(local_kernel, peers, planes, staps, per_group),
        grid=(channels // width,),
        in_specs=[smem, smem, whole(groups, taps), tiled(width, 3, staps), tiled(width, count, 3, length)]
        + [tiled(width, payload)] * peers,
        out_specs=[tiled(width, count, length)] * 2,
        out_shape=[jax.ShapeDtypeStruct((count, length, channels), F32)] * 2,
        scratch_shapes=[
            pltpu.VMEM((count * 3 * 8, peers * padded), BF16),
            pltpu.VMEM((groups * length, LANES), F32),
            pltpu.VMEM((groups * length, LANES), BF16),
            pltpu.VMEM((2 * count * 3 * (8 + length), LANES), F32),
        ],
        compiler_params=params,
        cost_estimate=cost(2 * count * 24 * peers * padded * channels, 14 * count * length * channels),
    )(me, stretch_owner, long_filter, weight, stretch, *sent)

    wide = min(1024, channels)
    return pl.pallas_call(
        functools.partial(finish_kernel, peers, cap, dpad),
        grid=(channels // wide,),
        in_specs=[smem, smem, smem] + [vmem] * (2 + 2 * peers),
        out_specs=[tiled(wide, count, length), tiled(wide, decode_count)],
        out_shape=[
            jax.ShapeDtypeStruct((count, length, channels), BF16),
            jax.ShapeDtypeStruct((decode_count, channels), BF16),
        ],
        scratch_shapes=[
            pltpu.VMEM((peers * cap, length, wide), BF16),
            pltpu.SMEM((count,), jnp.int32),
            pltpu.VMEM((decode_count, peers * dpad), BF16),
        ],
        compiler_params=params,
        cost_estimate=cost(3 * count * length * channels, 14 * count * length * channels),
    )(me, stretch_owner, row_owner, query, conv, *states, *returned)


def solution(mesh):
    placed = (
        P(("groups", "ctx"), None, None, "chan"),
        P(("groups", "ctx")),
        P(("groups", "ctx"), None, None),
        P(("groups", "ctx"), None, "chan"),
        P(("groups", "ctx")),
        P(("groups", "ctx")),
        P(("groups", "ctx"), None, None, "chan"),
        P(("groups", "ctx"), None, "chan"),
        P(None, None, "chan"),
        P("chan", None),
    )
    return jax.shard_map(
        per_device,
        mesh=mesh,
        in_specs=placed,
        out_specs=(P(("groups", "ctx"), None, "chan"), P(("groups", "ctx"), "chan")),
        check_vma=False,
    )
```

```python
import functools

import jax
import jax.numpy as jnp
from jax import lax
from jax.experimental import pallas as pl
from jax.experimental.pallas import tpu as pltpu
from jax.sharding import PartitionSpec as P

LANES = 128
F32 = jnp.float32
BF16 = jnp.bfloat16


def round_up(value, unit):
    return (value + unit - 1) // unit * unit


def one_hot(left, right):
    return jnp.where(left == right, 1.0, 0.0).astype(BF16)


def dot(left, right):
    return jnp.dot(left, right, preferred_element_type=F32)


def iota(shape, axis):
    return lax.broadcasted_iota(jnp.int32, shape, axis)


def rank_of(owner_ref, index):
    rank = jnp.int32(0)
    for earlier in range(index):
        rank += (owner_ref[earlier] == owner_ref[index]).astype(jnp.int32)
    return rank


def pick_own_group(stacked, length, per_group):
    lane_group = lax.rem(iota((length, stacked.shape[1]), 1), LANES) // per_group
    picked = stacked[:length]
    for group in range(1, LANES // per_group):
        picked = jnp.where(lane_group == group, stacked[group * length : (group + 1) * length], picked)
    return picked


def pack_kernel(ks, cap, planes, slots, dpad, me_ref, slot_hbm, owner_hbm, code_hbm, raw_hbm, rows_hbm, *rest):
    outs, rest = rest[: len(ks)], rest[len(ks) :]
    slot_ref, owner_ref, code_ref, raw_ref, rows_ref, out_ref, raw_sel, rows_sel, sems = rest
    padded = raw_sel.shape[0] // len(ks)
    decode_count = owner_ref.shape[0]
    channels = raw_ref.shape[1]
    piece = min(1024, channels)
    spans = [pl.ds(start, piece) for start in range(0, channels, piece)]
    pairs = [(slot_hbm, slot_ref), (owner_hbm, owner_ref), (code_hbm, code_ref)]
    for lanes in spans:
        pairs += [(raw_hbm.at[:, lanes], raw_ref.at[:, lanes]), (rows_hbm.at[:, lanes], rows_ref.at[:, lanes])]
    copies = [pltpu.make_async_copy(source, target, sems.at[at]) for at, (source, target) in enumerate(pairs)]
    for copy in copies:
        copy.start()
    for copy in copies[:3]:
        copy.wait()

    row = iota((padded, 1), 0)
    column = iota((padded, planes * slots), 1)
    lane = iota((1, 3 * decode_count), 1)
    wide = iota((1, LANES), 1)
    codes, places = [], []
    for at, k in enumerate(ks):
        peer = me_ref[0] ^ k
        target = jnp.full((padded, 1), -1, jnp.int32)
        for r in range(cap):
            slot = jnp.maximum(slot_ref[0, peer, r], 0)
            here = (row >= r * planes) & (row < (r + 1) * planes)
            target = jnp.where(here, (row - r * planes) * slots + slot, target)
        raw_sel[at * padded : (at + 1) * padded, :] = one_hot(column, target)
        target = jnp.full((1, 3 * decode_count), -1, jnp.int32)
        code = jnp.full((1, LANES), -1, jnp.int32)
        rank = jnp.int32(0)
        for n in range(decode_count):
            mine = owner_ref[n] == peer
            for s in range(3):
                hit = jnp.where(mine, s * decode_count + n, -1)
                target = jnp.where(lane == hit, rank + s * dpad, target)
            code = jnp.where(wide == jnp.where(mine, rank, -1), code_ref[n], code)
            rank += mine.astype(jnp.int32)
        places.append(one_hot(iota((3 * dpad, 3 * decode_count), 0), target).astype(F32))
        codes.append(code.astype(F32))

    rows_sel[...] = jnp.concatenate(places, axis=0).astype(BF16)
    marked = iota((padded, LANES), 0) == cap * planes
    leaving = []
    for step, lanes in enumerate(spans):
        copies[3 + 2 * step].wait()
        copies[4 + 2 * step].wait()
        picked = dot(raw_sel[...], raw_ref[:, lanes])
        placed = dot(rows_sel[...], rows_ref[:, lanes])
        for at in range(len(ks)):
            raw = picked[at * padded : (at + 1) * padded]
            if step == 0:
                head = jnp.where(marked, codes[at], raw[:, :LANES])
                raw = jnp.concatenate([head, raw[:, LANES:]], axis=1)
            rows = placed[at * 3 * dpad : (at + 1) * 3 * dpad]
            out_ref[at, :, lanes] = jnp.concatenate([raw, rows], axis=0).astype(BF16)
            sem = sems.at[len(copies) + len(leaving)]
            leaving.append(pltpu.make_async_copy(out_ref.at[at, :, lanes], outs[at].at[:, lanes], sem))
            leaving[-1].start()
    for copy in leaving:
        copy.wait()


def history_kernel(peers, cap, length, per_group, me_ref, slot_ref, filter_ref, hist_ref, *rest):
    sends, (first_ref, taps_ref) = rest[:peers], rest[peers : peers + 2]
    stage, toeplitz, local, states = rest[peers + 2 :]
    hist_rows, slots, _ = hist_ref.shape
    groups, taps = filter_ref.shape
    tile_rows = LANES // per_group * length

    @pl.when(pl.program_id(0) == 0)
    def _():
        source, column = iota((taps, LANES), 0), iota((taps, LANES), 1)
        for i in range(length):
            shift = jnp.where(column < hist_rows, one_hot(source, taps - 1 + i - column).astype(F32), 0.0)
            stage[pl.ds(i, groups, stride=length), :] = dot(filter_ref[...], shift.astype(BF16))
        toeplitz[...] = stage[: groups * length, :].astype(BF16)
        for i in range(length):
            stage[pl.ds(i, groups, stride=length), :] = dot(filter_ref[...], one_hot(source, i - column))
        local[...] = stage[: groups * length, :].astype(BF16)

    column0 = jnp.where(iota((LANES, LANES), 0) == 0, 1.0, 0.0).astype(BF16)
    tiles = hist_ref.shape[2] // LANES
    for tile in range(tiles):
        start = pl.multiple_of((pl.program_id(0) * tiles + tile) * tile_rows, tile_rows)
        lanes = slice(tile * LANES, (tile + 1) * LANES)
        expanded = dot(local[pl.ds(start, tile_rows), :], column0)
        taps_ref[:, lanes] = pick_own_group(expanded, length, per_group)
        matrix = toeplitz[pl.ds(start, tile_rows), :]
        block = hist_ref[:, :, lanes]
        rest_rows = jnp.zeros((LANES - hist_rows, slots, LANES), BF16)
        by_slot = jnp.swapaxes(jnp.concatenate([block, rest_rows], axis=0), 0, 1)
        for slot in range(0, slots, 2):
            pair = jnp.concatenate([by_slot[slot], by_slot[slot + 1]], axis=1)
            picked = pick_own_group(dot(matrix, pair), length, per_group)
            for e in range(2):
                own = picked[:, e * LANES : (e + 1) * LANES]
                states[slot + e, :, lanes] = own.astype(BF16)
                first_ref[slot + e : slot + e + 1, lanes] = own[:1]
    for k in range(peers):
        for r in range(cap):
            sends[k][r] = states[jnp.maximum(slot_ref[0, me_ref[0] ^ k, r], 0)]


def decode_kernel(peers, staps, slots, dpad, mark, padded, weight_ref, raw_ref, first_ref, taps_ref, *rest):
    rows, codes, outs = rest[:peers], rest[peers : 2 * peers], rest[2 * peers :]
    lane = iota((slots, LANES), 0)
    selects = []
    for ref in codes:
        code = ref[...].astype(F32)[mark : mark + 1].astype(jnp.int32)
        selects.append(jnp.where(lane == code, 1.0, 0.0).T[:dpad])
    select = jnp.concatenate(selects, axis=0)
    arrived = [ref[...].astype(F32)[padded:] for ref in rows]
    weight = weight_ref[...].astype(F32)
    featured = []
    for s in range(3):
        own = jnp.concatenate([block[s * dpad : (s + 1) * dpad] for block in arrived], axis=0)
        value = weight[s, 0:1] * own
        for j in range(1, staps):
            plane = (staps - 1 - j) * 3 + s
            state = dot(select.astype(BF16), raw_ref[plane * slots : (plane + 1) * slots, :])
            value += weight[s, j : j + 1] * state
        featured.append(value)
    gated = (featured[1] * featured[2]).astype(BF16).astype(F32)
    history = jnp.dot(select, first_ref[...], preferred_element_type=F32, precision=lax.Precision.HIGHEST)
    result = featured[0] * (taps_ref[0:1, :] * gated + history)
    for k in range(peers):
        outs[k][...] = result[k * dpad : (k + 1) * dpad].astype(BF16)


def local_kernel(peers, planes, staps, per_group, me_ref, owner_ref, filter_ref, weight_ref, rows_ref, *rest):
    raws, (query_ref, conv_ref) = rest[:peers], rest[peers : peers + 2]
    select, stage, local, window = rest[peers + 2 :]
    count, _, length, _ = rows_ref.shape
    groups, taps = filter_ref.shape
    padded = select.shape[1] // peers
    tile_rows = LANES // per_group * length
    lead = 8
    span = lead + length

    @pl.when(pl.program_id(0) == 0)
    def _():
        source, column = iota((taps, LANES), 0), iota((taps, LANES), 1)
        for i in range(length):
            stage[pl.ds(i, groups, stride=length), :] = dot(filter_ref[...], one_hot(source, i - column))
        local[...] = stage[...].astype(BF16)
        row = iota((lead, 1), 0) - (lead - staps + 1)
        targets = []
        for c in range(count):
            base = (owner_ref[c] ^ me_ref[0]) * padded + rank_of(owner_ref, c) * planes
            targets += [jnp.where(row >= 0, base + row * 3 + s, -1) for s in range(3)]
        select[...] = one_hot(iota(select.shape, 1), jnp.concatenate(targets, axis=0))

    lead_rows = dot(select[...], jnp.concatenate([ref[...][:padded] for ref in raws], axis=0))
    weights = weight_ref[...].astype(F32)
    tiles = rows_ref.shape[3] // LANES
    for tile in range(tiles):
        start = pl.multiple_of((pl.program_id(0) * tiles + tile) * tile_rows, tile_rows)
        lanes = slice(tile * LANES, (tile + 1) * LANES)
        matrix = local[pl.ds(start, tile_rows), :][:, :length]
        weight = weights[:, :, lanes]
        for first in range(0, count, 2):
            members = range(first, min(first + 2, count))
            products = []
            for c in members:
                featured = []
                for s in range(3):
                    base = (((tile % 2) * count + c) * 3 + s) * span
                    at = (c * 3 + s) * lead
                    window[base : base + lead, :] = lead_rows[at : at + lead, lanes]
                    window[base + lead : base + span, :] = rows_ref[c, s, :, lanes].astype(F32)
                    value = weight[s, 0:1] * window[base + lead : base + span, :]
                    for j in range(1, staps):
                        value += weight[s, j : j + 1] * window[base + lead - j : base + span - j, :]
                    featured.append(value)
                query_ref[c, :, lanes] = featured[0]
                products.append((featured[1] * featured[2]).astype(BF16))
            picked = pick_own_group(dot(matrix, jnp.concatenate(products, axis=1)), length, per_group)
            for e, c in enumerate(members):
                conv_ref[c, :, lanes] = picked[:, e * LANES : (e + 1) * LANES]


def finish_kernel(peers, cap, dpad, me_ref, owner_ref, decode_owner_ref, query_ref, conv_ref, *rest):
    states, returned = rest[:peers], rest[peers : 2 * peers]
    out_ref, decode_ref, held, places, select = rest[2 * peers :]
    count, length, width = out_ref.shape
    decode_count = decode_owner_ref.shape[0]

    @pl.when(pl.program_id(0) == 0)
    def _():
        for c in range(count):
            places[c] = (owner_ref[c] ^ me_ref[0]) * cap + rank_of(owner_ref, c)
        row = iota((decode_count, 1), 0)
        target = jnp.zeros((decode_count, 1), jnp.int32)
        for n in range(decode_count):
            at = (decode_owner_ref[n] ^ me_ref[0]) * dpad + rank_of(decode_owner_ref, n)
            target = jnp.where(row == n, at, target)
        select[...] = one_hot(iota((decode_count, peers * dpad), 1), target)

    lanes = pl.ds(pl.multiple_of(pl.program_id(0) * width, width), width)
    for k in range(peers):
        for r in range(cap):
            held[k * cap + r] = states[k][r, :, lanes]
    for c in range(count):
        state = held[places[c]].astype(F32)
        out_ref[c] = (query_ref[c, :, lanes] * (conv_ref[c, :, lanes] + state)).astype(BF16)
    arrived = jnp.concatenate([ref[:, lanes].astype(F32) for ref in returned], axis=0).astype(BF16)
    decode_ref[...] = dot(select[...], arrived).astype(BF16)


def per_device(
    stretch_rows,
    stretch_owner,
    send_slot,
    decode_rows,
    row_owner,
    row_slot,
    cache_raw,
    cache_hist,
    short_weight,
    long_filter,
):
    peers = lax.axis_size("ctx")
    cap = send_slot.shape[2]
    count, length, _, channels = stretch_rows.shape
    slots, raw_rows, _, _ = cache_raw.shape
    hist_rows = cache_hist.shape[1]
    staps = short_weight.shape[0]
    groups, taps = long_filter.shape
    per_group = channels // groups
    decode_count = decode_rows.shape[0]
    dcap = max(2, (2 * decode_count + peers - 1) // peers)
    dpad = round_up(dcap, 8)
    planes = 3 * raw_rows
    padded = round_up(planes * cap + 1, 16)
    me = lax.axis_index("ctx").astype(jnp.int32).reshape(1)

    raw2d = cache_raw.transpose(1, 2, 0, 3).reshape(planes * slots, channels)
    hist3d = cache_hist.transpose(1, 0, 2)
    rows2d = decode_rows.transpose(1, 0, 2).reshape(3 * decode_count, channels)
    stretch = stretch_rows.transpose(0, 2, 1, 3)
    weight = short_weight.transpose(1, 0, 2)

    smem = pl.BlockSpec(memory_space=pltpu.SMEM)
    vmem = pl.BlockSpec(memory_space=pltpu.VMEM)
    hbm = pl.BlockSpec(memory_space=pltpu.HBM)
    params = pltpu.CompilerParams(vmem_limit_bytes=24 * 1024 * 1024)

    def tiled(width, *lead):
        return pl.BlockSpec((*lead, width), lambda t: (0,) * len(lead) + (t,))

    def whole(*shape):
        return pl.BlockSpec(shape, lambda t: (0,) * len(shape))

    def cost(flops, data):
        return pl.CostEstimate(flops=1, bytes_accessed=1, transcendentals=0)

    def send(array, k):
        return lax.ppermute(array, "ctx", [(i, i ^ k) for i in range(peers)])

    order = sorted(range(1, peers), reverse=True)
    width = min(512, channels)
    payload = padded + 3 * dpad
    sent = [None] * peers

    def pack(ks, limit, raw_in, rows_in):
        packed = pl.pallas_call(
            functools.partial(pack_kernel, ks, cap, planes, slots, dpad),
            in_specs=[smem] + [hbm] * 5,
            out_specs=[hbm] * len(ks),
            out_shape=[jax.ShapeDtypeStruct((payload, channels), BF16)] * len(ks),
            scratch_shapes=[
                pltpu.SMEM(send_slot.shape, jnp.int32),
                pltpu.SMEM(row_owner.shape, jnp.int32),
                pltpu.SMEM(row_slot.shape, jnp.int32),
                pltpu.VMEM((planes * slots, channels), BF16),
                pltpu.VMEM((3 * decode_count, channels), BF16),
                pltpu.VMEM((len(ks), payload, channels), BF16),
                pltpu.VMEM((len(ks) * padded, planes * slots), BF16),
                pltpu.VMEM((len(ks) * 3 * dpad, 3 * decode_count), BF16),
                pltpu.SemaphoreType.DMA((3 + (2 + len(ks)) * -(-channels // 1024),)),
            ],
            compiler_params=pltpu.CompilerParams(vmem_limit_bytes=limit * 1024 * 1024),
            cost_estimate=cost(2 * len(ks) * padded * planes * slots * channels, 4 * planes * slots * channels),
        )(me, send_slot, row_owner, row_slot, raw_in, rows_in)
        for k, block in zip(ks, packed):
            sent[k] = send(block, k) if k else block

    pack(order[:-1], 60, raw2d, rows2d)

    tile_rows = LANES // per_group * length
    history = pl.pallas_call(
        functools.partial(history_kernel, peers, cap, length, per_group),
        grid=(channels // width,),
        in_specs=[smem, smem, whole(groups, taps), tiled(width, hist_rows, slots)],
        out_specs=[tiled(width, cap, length)] * peers + [tiled(width, slots), tiled(width, length)],
        out_shape=[jax.ShapeDtypeStruct((cap, length, channels), BF16)] * peers
        + [jax.ShapeDtypeStruct((slots, channels), F32), jax.ShapeDtypeStruct((length, channels), F32)],
        scratch_shapes=[
            pltpu.VMEM((groups * length, LANES), F32),
            pltpu.VMEM((groups * length, LANES), BF16),
            pltpu.VMEM((groups * length, LANES), BF16),
            pltpu.VMEM((slots, length, width), BF16),
        ],
        compiler_params=pltpu.CompilerParams(vmem_limit_bytes=48 * 1024 * 1024),
        cost_estimate=cost(2 * slots * tile_rows * LANES * channels, 2 * hist_rows * slots * channels),
    )(me, send_slot, long_filter, hist3d)
    states, (first, expanded) = list(history[:peers]), history[peers:]
    raw_in, rows_in, first = lax.optimization_barrier((raw2d, rows2d, first))
    pack([1, 0], 32, raw_in, rows_in)
    for k in order:
        states[k] = send(states[k], k)

    returned = list(
        pl.pallas_call(
            functools.partial(decode_kernel, peers, staps, slots, dpad, planes * cap, padded),
            grid=(channels // width,),
            in_specs=[tiled(width, 3, staps), tiled(width, planes * slots), tiled(width, slots)]
            + [tiled(width, length)]
            + [tiled(width, payload)] * peers
            + [whole(payload, LANES)] * peers,
            out_specs=[tiled(width, dpad)] * peers,
            out_shape=[jax.ShapeDtypeStruct((dpad, channels), BF16)] * peers,
            compiler_params=params,
            cost_estimate=cost(2 * peers * dpad * planes * slots * channels, 4 * planes * slots * channels),
        )(weight, raw2d, first, expanded, *sent, *sent)
    )
    for k in order:
        returned[k] = send(returned[k], k)

    query, conv = pl.pallas_call(
        functools.partial(local_kernel, peers, planes, staps, per_group),
        grid=(channels // width,),
        in_specs=[smem, smem, whole(groups, taps), tiled(width, 3, staps), tiled(width, count, 3, length)]
        + [tiled(width, payload)] * peers,
        out_specs=[tiled(width, count, length)] * 2,
        out_shape=[jax.ShapeDtypeStruct((count, length, channels), F32)] * 2,
        scratch_shapes=[
            pltpu.VMEM((count * 3 * 8, peers * padded), BF16),
            pltpu.VMEM((groups * length, LANES), F32),
            pltpu.VMEM((groups * length, LANES), BF16),
            pltpu.VMEM((2 * count * 3 * (8 + length), LANES), F32),
        ],
        compiler_params=params,
        cost_estimate=cost(2 * count * 24 * peers * padded * channels, 14 * count * length * channels),
    )(me, stretch_owner, long_filter, weight, stretch, *sent)

    wide = min(1024, channels)
    return pl.pallas_call(
        functools.partial(finish_kernel, peers, cap, dpad),
        grid=(channels // wide,),
        in_specs=[smem, smem, smem] + [vmem] * (2 + 2 * peers),
        out_specs=[tiled(wide, count, length), tiled(wide, decode_count)],
        out_shape=[
            jax.ShapeDtypeStruct((count, length, channels), BF16),
            jax.ShapeDtypeStruct((decode_count, channels), BF16),
        ],
        scratch_shapes=[
            pltpu.VMEM((peers * cap, length, wide), BF16),
            pltpu.SMEM((count,), jnp.int32),
            pltpu.VMEM((decode_count, peers * dpad), BF16),
        ],
        compiler_params=params,
        cost_estimate=cost(3 * count * length * channels, 14 * count * length * channels),
    )(me, stretch_owner, row_owner, query, conv, *states, *returned)


def solution(mesh):
    placed = (
        P(("groups", "ctx"), None, None, "chan"),
        P(("groups", "ctx")),
        P(("groups", "ctx"), None, None),
        P(("groups", "ctx"), None, "chan"),
        P(("groups", "ctx")),
        P(("groups", "ctx")),
        P(("groups", "ctx"), None, None, "chan"),
        P(("groups", "ctx"), None, "chan"),
        P(None, None, "chan"),
        P("chan", None),
    )
    return jax.shard_map(
        per_device,
        mesh=mesh,
        in_specs=placed,
        out_specs=(P(("groups", "ctx"), None, "chan"), P(("groups", "ctx"), "chan")),
        check_vma=False,
    )
```
